32 devices in a mesh: clips: 8 (over z, y), seq: 4 (over x, core).
Axes of the slice: x: 2, y: 2, z: 4, core: 2. Of those that a mesh axis runs over, the one named last changes fastest.
Arguments:
- frames_in: bfloat16 [32, 256, 1024], P('clips', 'seq'), may hold values from -6 to 6
- output_grad: bfloat16 [32, 256, 1024], P('clips', 'seq'), may hold values from -6 to 6
- clip_kinds: int32 [32], P('clips'), may hold values from 0 to 1, as said below
- clip_lengths: int32 [32], P('clips'), may hold values from 110 to 250, as said below
- norm1_gain: bfloat16 [1024], P(('clips', 'seq')), may hold values from 0.5 to 1.5
- norm1_bias: bfloat16 [1024], P(('clips', 'seq')), may hold values from -3 to 3
- w_qkv: bfloat16 [1024, 3072], P(('clips', 'seq')), may hold values from -0.1875 to 0.1875
- w_out: bfloat16 [1024, 1024], P(('clips', 'seq')), may hold values from -2 to 2
- attn_scale: bfloat16 [1024], P(('clips', 'seq')), may hold values from 0.25 to 1.75
- norm2_gain: bfloat16 [1024], P(('clips', 'seq')), may hold values from 0.5 to 1.5
- norm2_bias: bfloat16 [1024], P(('clips', 'seq')), may hold values from -3 to 3
- w_gate_up: bfloat16 [1024, 8192], P(('clips', 'seq')), may hold values from -0.1875 to 0.1875
- w_down: bfloat16 [4096, 1024], P(('clips', 'seq')), may hold values from -0.1875 to 0.1875
- mlp_scale: bfloat16 [1024], P(('clips', 'seq')), may hold values from 0.25 to 1.75
Outputs:
- layer_output: bfloat16 [32, 256, 1024], P('clips', 'seq')
- input_grad: float32 [32, 256, 1024], P('clips', 'seq')
- grad_norm1_gain: float32 [1024], P(('clips', 'seq'))
- grad_norm1_bias: float32 [1024], P(('clips', 'seq'))
- grad_w_qkv: float32 [1024, 3072], P(('clips', 'seq'))
- grad_w_out: float32 [1024, 1024], P(('clips', 'seq'))
- grad_attn_scale: float32 [1024], P(('clips', 'seq'))
- grad_norm2_gain: float32 [1024], P(('clips', 'seq'))
- grad_norm2_bias: float32 [1024], P(('clips', 'seq'))
- grad_w_gate_up: float32 [1024, 8192], P(('clips', 'seq'))
- grad_w_down: float32 [4096, 1024], P(('clips', 'seq'))
- grad_mlp_scale: float32 [1024], P(('clips', 'seq'))
The draws below stay inside these ranges and needn't reach their ends.
Inputs may be any that keep to these rules, and one draw needn't show every extreme that they name: `clip_kinds`: each aligned block of 4 clips holds at least one clip of kind 0. `clip_lengths`: A clip of kind 0 has 235 to 250 frames, one of kind 1 has 110 to 125; each aligned block of 4 clips holds a clip of kind 0 with 250 frames.
All inputs are finite; a program needn't handle non-finite values.
Results may differ from the reference program's by a relative error of at most 0.019.
Values may be sent and summed in bfloat16 or wider, within the bound.
No kernel may reach another device: no remote copies, remote signals or barrier semaphores. Data moves between devices by JAX's collectives and lax.ppermute only.
A program may use at most 192 MiB of HBM per device.

```python
import jax
import jax.numpy as jnp
from jax import lax

D = 1024
H = 16
HD = 64
FF = 4096
WIN = 128
L = 256
LEN_HI = 250
LEN_LO = 125
CLIPS_GRP = 4
CLIPS = 32


def clip_plan(key):
    kind_key, trim_key, pick_key = jax.random.split(key, 3)
    clip_kind = jax.random.randint(kind_key, (CLIPS,), 0, 2)
    trim_by = jax.random.randint(trim_key, (CLIPS,), 0, L // 16)
    chosen = jax.random.randint(pick_key, (CLIPS // CLIPS_GRP,), 0, CLIPS_GRP)
    clip_index = jnp.arange(CLIPS)
    forced = clip_index % CLIPS_GRP == jnp.repeat(chosen, CLIPS_GRP)
    clip_kind = jnp.where(forced, 0, clip_kind)
    lengths = jnp.where(clip_kind == 0, LEN_HI - trim_by, LEN_LO - trim_by)
    lengths = jnp.where(forced, LEN_HI, lengths)
    return (clip_kind.astype(jnp.int32), lengths.astype(jnp.int32))


def draw_clip_kinds(key, part):
    return clip_plan(key)[0]


def draw_clip_lengths(key, part):
    return clip_plan(key)[1]


def level_of(stream_key, extent, cuts, least, top_value):
    loudness = 1.0
    for position, blocks in cuts:
        steps = jax.random.uniform(jax.random.fold_in(jax.random.fold_in(stream_key, 6), position), (blocks,), jnp.float32, least / len(cuts), top_value / len(cuts))
        loudness = loudness * jnp.repeat(jnp.exp(steps), extent[position] // blocks).reshape((-1,) + (1,) * (len(extent) - 1 - position))
    return loudness


def scatter_about(rng, shape, scale, most, cuts=(), held_as=jnp.bfloat16):
    values = jax.random.normal(rng, shape, jnp.float32) * scale
    if len(cuts) > 0:
        values = level_of(rng, shape, cuts, -0.22, 0.18) * values
    return jnp.clip(values, min=-most, max=most).astype(held_as)


def setup_inputs(seed: int = 0) -> dict:
    streams_of = jax.random.split(jax.random.key(seed), 15)
    frames_in = scatter_about(streams_of[0], (CLIPS, L, D), 1.0, 6.0, ((0, 8), (1, 4)))
    output_grad = scatter_about(streams_of[1], (CLIPS, L, D), 1.0, 6.0, ((0, 8), (1, 4)))
    clip_kinds = draw_clip_kinds(jax.random.fold_in(streams_of[14], 71), 0)
    clip_lengths = draw_clip_lengths(jax.random.fold_in(streams_of[14], 71), 0)
    norm1_gain = jnp.clip(1.0 + 0.1 * jax.random.normal(streams_of[4], (D,), jnp.float32), 0.5, 1.5).astype(jnp.bfloat16)
    norm1_bias = scatter_about(streams_of[5], (D,), 0.5, 3.0, ((0, 32),))
    w_qkv = scatter_about(streams_of[6], (D, 3 * D), D ** -0.5, 0.1875, ((0, 32),))
    w_out = scatter_about(streams_of[7], (D, D), (D // 128) ** -0.5, 2.0, ((0, 32),))
    attn_scale = jnp.clip(1.0 + 0.15 * jax.random.normal(streams_of[8], (D,), jnp.float32), 0.25, 1.75).astype(jnp.bfloat16)
    norm2_gain = jnp.clip(1.0 + 0.1 * jax.random.normal(streams_of[9], (D,), jnp.float32), 0.5, 1.5).astype(jnp.bfloat16)
    norm2_bias = scatter_about(streams_of[10], (D,), 0.5, 3.0, ((0, 32),))
    w_gate_up = scatter_about(streams_of[11], (D, 2 * FF), D ** -0.5, 0.1875, ((0, 32),))
    w_down = scatter_about(streams_of[12], (FF, D), (FF // 4) ** -0.5, 0.1875, ((0, 32),))
    mlp_scale = jnp.clip(1.0 + 0.15 * jax.random.normal(streams_of[13], (D,), jnp.float32), 0.25, 1.75).astype(jnp.bfloat16)
    return dict(frames_in=frames_in, output_grad=output_grad, clip_kinds=clip_kinds, clip_lengths=clip_lengths, norm1_gain=norm1_gain, norm1_bias=norm1_bias, w_qkv=w_qkv, w_out=w_out, attn_scale=attn_scale, norm2_gain=norm2_gain, norm2_bias=norm2_bias, w_gate_up=w_gate_up, w_down=w_down, mlp_scale=mlp_scale)


@jax.custom_vjp
def low(v):
    return lax.optimization_barrier(v.astype(jnp.bfloat16)).astype(jnp.float32)

@jax.custom_vjp
def low_back(v):
    return v

def low_keep(v):
    return (low(v), None)

def low_pass(kept, grad):
    return (grad,)

def back_keep(v):
    return (v, None)

def back_low(kept, grad):
    return (low(grad),)
low.defvjp(low_keep, low_pass)
low_back.defvjp(back_keep, back_low)
HIGHEST = lax.Precision.HIGHEST
NEG_FILL = -1000000000.0
EPS = 1e-05

def matmul_hi(left, right):
    return jnp.dot(left, right, precision=HIGHEST, preferred_element_type=jnp.float32)

def layer_norm(values, gain, shift):
    center = values - lax.optimization_barrier(jnp.mean(values, axis=-1, keepdims=True))
    spread = lax.optimization_barrier(jnp.mean(center * center, axis=-1, keepdims=True))
    return center * lax.rsqrt(spread + EPS) * gain + shift

def rotary_tables(positions, head_size):
    half_size = head_size // 2
    inv_freq = 10000.0 ** (-2.0 * jnp.arange(half_size).astype(jnp.float32) / head_size)
    angles = positions[..., None] * inv_freq
    return (jnp.cos(angles), jnp.sin(angles))

def rotate(values, cosine_table, sine_table):
    half_size = values.shape[-1] // 2
    first_half = values[..., :half_size]
    second_half = values[..., half_size:]
    return jnp.concatenate([first_half * cosine_table - second_half * sine_table, second_half * cosine_table + first_half * sine_table], axis=-1)

def band_bias(lengths, total):
    frame_index = jnp.arange(total)
    gap = jnp.abs(frame_index[:, None] - frame_index[None, :])
    visible = (gap <= WIN // 2)[None] & (frame_index[None, None, :] < lengths[:, None, None])
    return jnp.where(visible, 0.0, NEG_FILL).astype(jnp.float32)

def forward(input_block, params, clip_kind, lengths):
    gain_one, shift_one, w_qkv, w_out, scale_attn, gain_two, shift_two, w_gate_up, w_down, scale_mlp = params
    clip_count = input_block.shape[0]
    row_count = clip_count * L
    frame_index = jnp.arange(L)
    mask_rows = (frame_index[None, :] < lengths[:, None]).astype(jnp.float32).reshape(row_count, 1)
    positions = frame_index.astype(jnp.float32)[None, :] * (1.0 + clip_kind.astype(jnp.float32))[:, None]
    cosine_table, sine_table = rotary_tables(positions, HD)
    cosine_full = cosine_table[:, :, None, None, :]
    sine_full = sine_table[:, :, None, None, :]
    input_rows = input_block.reshape(row_count, D)
    act_one = low(layer_norm(input_rows, gain_one, shift_one))
    projected = low_back(matmul_hi(act_one, w_qkv)).reshape(clip_count, L, 3, H, HD)
    turned = rotate(projected[:, :, :2], cosine_full, sine_full)
    sectioned = low_back(low(jnp.concatenate([turned, projected[:, :, 2:]], axis=2)))
    queries = sectioned[:, :, 0]
    keys_in = sectioned[:, :, 1]
    values_in = sectioned[:, :, 2]
    scores = jnp.einsum('nihd,njhd->nhij', queries, keys_in, precision=HIGHEST) * HD ** (-0.5)
    scores = low_back(scores + band_bias(lengths, L)[:, None])
    weights = low(jax.nn.softmax(scores, axis=-1))
    mixed = jnp.einsum('nhij,njhd->nihd', weights, values_in, precision=HIGHEST)
    mixed = low_back(low(mixed)).reshape(row_count, D)
    attn_out = low_back(matmul_hi(mixed, w_out))
    resid = input_rows + mask_rows * scale_attn * attn_out
    act_two = low(layer_norm(resid, gain_two, shift_two))
    gate_up = low_back(matmul_hi(act_two, w_gate_up))
    hidden = low(jax.nn.silu(gate_up[:, :FF]) * gate_up[:, FF:])
    mlp_out = low_back(matmul_hi(hidden, w_down))
    return (resid + mask_rows * scale_mlp * mlp_out).reshape(input_block.shape)

def reference(frames_in, output_grad, clip_kinds, clip_lengths, norm1_gain, norm1_bias, w_qkv, w_out, attn_scale, norm2_gain, norm2_bias, w_gate_up, w_down, mlp_scale):
    params = tuple((weight_in.astype(jnp.float32) for weight_in in (norm1_gain, norm1_bias, w_qkv, w_out, attn_scale, norm2_gain, norm2_bias, w_gate_up, w_down, mlp_scale)))
    block_count = CLIPS // CLIPS_GRP
    input_blocks = frames_in.astype(jnp.float32).reshape(block_count, CLIPS_GRP, L, D)
    grad_blocks = output_grad.astype(jnp.float32).reshape(block_count, CLIPS_GRP, L, D)
    kind_blocks = clip_kinds.reshape(block_count, CLIPS_GRP)
    length_blocks = clip_lengths.reshape(block_count, CLIPS_GRP)

    def scan_step(totals, block_in):
        input_block, grad_block, kind_block, length_block = block_in
        out_block, pull = jax.vjp(lambda inputs, weights_in: forward(inputs, weights_in, kind_block, length_block), input_block, params)
        grad_input, grad_params = pull(grad_block)
        totals = jax.tree.map(jnp.add, totals, grad_params)
        return (totals, (out_block.astype(jnp.bfloat16), grad_input))
    zero_totals = jax.tree.map(jnp.zeros_like, params)
    grad_totals, (out_blocks, grad_inputs) = lax.scan(scan_step, zero_totals, (input_blocks, grad_blocks, kind_blocks, length_blocks))
    return (out_blocks.reshape(CLIPS, L, D), grad_inputs.reshape(CLIPS, L, D), grad_totals[0], grad_totals[1], grad_totals[2], grad_totals[3], grad_totals[4], grad_totals[5], grad_totals[6], grad_totals[7], grad_totals[8], grad_totals[9])
```

```python
import functools

import jax
import jax.numpy as jnp
import numpy as np
from jax import lax
from jax.experimental import pallas as pl
from jax.experimental.pallas import tpu as pltpu
from jax.sharding import Mesh
from jax.sharding import PartitionSpec as P

H = 16
HD = 64
FF = 4096
WIN = 128
NEG_FILL = -1000000000.0
EPS = 1e-05
BF = jnp.bfloat16
F32 = jnp.float32
VMEM_BYTES = 56 * 1024 * 1024

ID_SEQ, ID_Y, ID_POS, ID_GPOS, ID_DEST, ID_CPOS = 0, 1, 2, 10, 14, 18


def dot_nn(left, right):
    return jnp.dot(left, right, preferred_element_type=F32)


def dot_nt(left, right):
    return lax.dot_general(left, right, (((1,), (1,)), ((), ())), preferred_element_type=F32)


def dot_tn(left, right):
    return lax.dot_general(left, right, (((0,), (0,)), ((), ())), preferred_element_type=F32)


def smem():
    return pl.BlockSpec(memory_space=pltpu.SMEM)


def vmem():
    return pl.BlockSpec(memory_space=pltpu.VMEM)


def shaped(shape, dtype):
    return jax.ShapeDtypeStruct(shape, dtype)


def params():
    return pltpu.CompilerParams(vmem_limit_bytes=VMEM_BYTES)


def cost(flops, moved):
    return pl.CostEstimate(flops=int(flops), bytes_accessed=int(moved), transcendentals=0)


def rows_at(index, size):
    return pl.ds(pl.multiple_of(index * size, size), size)


def normed(values):
    center = values - jnp.mean(values, axis=-1, keepdims=True)
    spread = lax.rsqrt(jnp.mean(center * center, axis=-1, keepdims=True) + EPS)
    return center * spread, spread


def norm_one_kernel(x0, x1, x2, x3, vecs, act):
    gain, shift = vecs[0:1, :], vecs[1:2, :]
    for slot, frames in enumerate((x0, x1, x2, x3)):
        xhat, _ = normed(frames[...].astype(F32))
        act[slot] = (xhat * gain + shift).astype(BF)


def visible_bias(fcol, frow, length):
    gap = jnp.abs(fcol[...] - frow[...])
    seen = (gap <= WIN // 2) & (frow[...] < length.astype(F32))
    return jnp.where(seen, 0.0, NEG_FILL)


def turn(values, cosine, sine, lower):
    swapped = jnp.where(lower, pltpu.roll(values, 96, 1), pltpu.roll(values, 32, 1))
    return values * cosine + swapped * sine


def lane_masks():
    lane = lax.broadcasted_iota(jnp.int32, (1, 128), 1)
    lower = lane % 64 < 32
    return lower, [(lane // 64 == half).astype(F32) for half in (0, 1)]


def attend_kernel(ids, lens, act, *refs):
    pieces, (cosine, sine, fcol, frow, sect, weight, m0, m1, m2, m3) = refs[:8], refs[8:]
    clip = pl.program_id(0)

    @pl.when(clip == 0)
    def _():
        for place, piece in enumerate(pieces):
            weight[rows_at(ids[ID_POS + place], 128), :] = piece[...]

    rows = act.shape[0] * act.shape[2]
    slab = act.shape[2]
    projected = dot_nn(act[...].reshape(rows, act.shape[3]), weight[...])
    cos_rows = cosine[...].reshape(rows, 128)
    sin_rows = sine[...].reshape(rows, 128)
    lower, masks = lane_masks()
    lower = jnp.broadcast_to(lower, (rows, 128))
    chunks = []
    for place in range(6):
        chunk = projected[:, 128 * place : 128 * place + 128]
        if place < 4:
            chunk = turn(chunk, cos_rows, sin_rows, lower)
        chunk = chunk.astype(BF)
        chunks.append(chunk)
        sect[:, 0, :, 128 * place : 128 * place + 128] = chunk.reshape(-1, slab, 128)
    bias = visible_bias(fcol, frow, lens[clip])
    for pair in range(2):
        total = jnp.zeros((rows, 128), F32)
        for half in range(2):
            mask = masks[half].astype(BF)
            scores = dot_nt(chunks[pair] * mask, chunks[2 + pair]) * HD ** (-0.5) + bias
            expo = jnp.exp(scores - jnp.max(scores, axis=-1, keepdims=True))
            weights = (expo / jnp.sum(expo, axis=-1, keepdims=True)).astype(BF)
            total = total + dot_nn(weights, chunks[4 + pair] * mask)
        total = total.astype(BF)
        for slot, out in enumerate((m0, m1, m2, m3)):
            out[0, :, 128 * pair : 128 * pair + 128] = total[slab * slot : slab * (slot + 1)]


def attend_back_kernel(lens, sect, g0, g1, g2, g3, cosine, sine, fcol, frow, grad):
    clip = pl.program_id(0)
    slab = sect.shape[2]
    rows = sect.shape[0] * slab
    cos_rows = cosine[...].reshape(rows, 128)
    sin_rows = -sine[...].reshape(rows, 128)
    lower, masks = lane_masks()
    lower = jnp.broadcast_to(lower, (rows, 128))
    bias = visible_bias(fcol, frow, lens[clip])

    def part(place):
        return sect[:, 0, :, 128 * place : 128 * place + 128].reshape(rows, 128)

    def put(place, values):
        grad[:, 0, :, 128 * place : 128 * place + 128] = values.astype(BF).reshape(-1, slab, 128)

    for pair in range(2):
        queries, keys_in, values_in = part(pair), part(2 + pair), part(4 + pair)
        mixed_grad = jnp.concatenate(
            [g[0, :, 128 * pair : 128 * pair + 128] for g in (g0, g1, g2, g3)], axis=0
        )
        grad_q = jnp.zeros((rows, 128), F32)
        grad_k = jnp.zeros((rows, 128), F32)
        grad_v = jnp.zeros((rows, 128), F32)
        for half in range(2):
            mask = masks[half].astype(BF)
            query = queries * mask
            upper = mixed_grad * mask
            scores = dot_nt(query, keys_in) * HD ** (-0.5) + bias
            expo = jnp.exp(scores - jnp.max(scores, axis=-1, keepdims=True))
            probs = expo / jnp.sum(expo, axis=-1, keepdims=True)
            grad_v = grad_v + dot_tn(probs.astype(BF), upper)
            grad_probs = dot_nt(upper, values_in)
            centre = jnp.sum(probs * grad_probs, axis=-1, keepdims=True)
            grad_scores = (probs * (grad_probs - centre)).astype(BF)
            grad_q = grad_q + dot_nn(grad_scores, keys_in * mask)
            grad_k = grad_k + dot_tn(grad_scores, query)
        grad_q = (grad_q * HD ** (-0.5)).astype(BF).astype(F32)
        grad_k = (grad_k * HD ** (-0.5)).astype(BF).astype(F32)
        put(pair, turn(grad_q, cos_rows, sin_rows, lower))
        put(2 + pair, turn(grad_k, cos_rows, sin_rows, lower))
        put(4 + pair, grad_v)


def middle_kernel(
    ids, m0, m1, m2, m3, w0, w1, w2, w3, frames, mask, vecs, weight, attn_out, resid, act
):
    me = ids[ID_SEQ]
    for slot, packed in enumerate((w0, w1, w2, w3)):
        other = jnp.bitwise_xor(me, slot)
        for place in range(8):
            start = pl.multiple_of(ids[ID_POS + place] * 128 + other * 32, 32)
            for quarter in range(4):
                weight[pl.ds(start, 32), 256 * quarter : 256 * quarter + 256] = packed[
                    place, 32 * quarter : 32 * quarter + 32, :
                ]
    total = jnp.zeros(attn_out.shape, F32)
    for slot, mixed in enumerate((m0, m1, m2, m3)):
        block = weight[rows_at(jnp.bitwise_xor(me, slot), 256), :]
        total = total + dot_nn(mixed[...], block)
    attn_out[...] = total
    summed = frames[...].astype(F32) + mask[...] * vecs[2:3, :] * total
    resid[...] = summed
    xhat, _ = normed(summed)
    act[...] = (xhat * vecs[3:4, :] + vecs[4:5, :]).astype(BF)


def middle_back_kernel(
    ids, q0, q1, q2, q3, resid, attn_out, grad_in, mask, vecs, weight,
    grad_resid, grad_attn, g0, g1, g2, g3, sums,
):
    me = ids[ID_SEQ]
    grad_act = q0[...].astype(F32) + q1[...].astype(F32) + q2[...].astype(F32) + q3[...].astype(F32)
    xhat, spread = normed(resid[...])
    sums[0:1, :] = jnp.sum(grad_act * xhat, axis=0, keepdims=True)
    sums[1:2, :] = jnp.sum(grad_act, axis=0, keepdims=True)
    pulled = grad_act * vecs[3:4, :]
    pulled = spread * (
        pulled
        - jnp.mean(pulled, axis=-1, keepdims=True)
        - xhat * jnp.mean(pulled * xhat, axis=-1, keepdims=True)
    )
    total = grad_in[...].astype(F32) + pulled
    grad_resid[...] = total
    masked = mask[...] * total
    sums[2:3, :] = jnp.sum(masked * attn_out[...], axis=0, keepdims=True)
    sums[3:8, :] = jnp.zeros((5, sums.shape[1]), F32)
    scaled = (masked * vecs[2:3, :]).astype(BF)
    grad_attn[...] = scaled
    for slot, out in enumerate((g0, g1, g2, g3)):
        block = weight[rows_at(jnp.bitwise_xor(me, slot), 256), :]
        out[...] = dot_nt(scaled, block).astype(BF)


def out_grad_kernel(ids, m0, m1, m2, m3, grad_attn, o0, o1, o2, o3, held):
    me = ids[ID_SEQ]
    for slot, mixed in enumerate((m0, m1, m2, m3)):
        held[rows_at(jnp.bitwise_xor(me, slot), 256), :] = dot_tn(mixed[...], grad_attn[...]).astype(
            BF
        )
    for slot, out in enumerate((o0, o1, o2, o3)):
        other = jnp.bitwise_xor(me, slot)
        for place in range(8):
            start = pl.multiple_of(ids[ID_CPOS + place] * 128 + other * 32, 32)
            out[place] = held[pl.ds(start, 32), :]


def mlp_kernel(
    ids, a0, a1, o0, o1, p0, p1, p2, p3, vecs, hidden, grads, grad_mlp, even, odd, w_in, w_down
):
    for place, piece in enumerate((p0, p1, p2, p3)):
        block = ids[ID_GPOS + place]
        w_in[rows_at(block, 256), :] = piece[0:256, :]
        w_down[rows_at(block, 128), :] = piece[256:384, :]
    width = hidden.shape[1]
    for slot, (act, seed, out) in enumerate(((a0, o0, even), (a1, o1, odd))):
        here = slice(256 * slot, 256 * slot + 256)
        gate_up = dot_nn(act[...], w_in[...])
        gate, up = gate_up[:, :width], gate_up[:, width:]
        pulled = (vecs[5:6, :] * seed[...].astype(F32)).astype(BF)
        grad_mlp[here, :] = pulled
        grad_hidden = dot_nt(pulled, w_down[...])
        sig = jax.nn.sigmoid(gate)
        silu = gate * sig
        hidden[here, :] = (silu * up).astype(BF)
        grad_gate = grad_hidden * up * sig * (1.0 + gate * (1.0 - sig))
        grads[here, :width] = grad_gate.astype(BF)
        grads[here, width:] = (grad_hidden * silu).astype(BF)
        out[...] = dot_nt(grads[here, :], w_in[...]).astype(BF)


def mlp_grad_kernel(places, ids, *refs):
    acts, refs = refs[:8], refs[8:]
    grads, refs = refs[:4], refs[4:]
    hidden, refs = refs[:4], refs[4:]
    grad_mlp, outs = refs[:4], refs[4:]
    for place, out in zip(places, outs):
        block = ids[ID_DEST + place]
        wide = pl.ds(pl.multiple_of(block * 256, 256), 256)
        narrow = pl.ds(pl.multiple_of(block * 128, 128), 128)
        upper = jnp.zeros((256, out.shape[1]), F32)
        lower = jnp.zeros((128, out.shape[1]), F32)
        for pair in range(4):
            for slot in range(2):
                here = slice(256 * slot, 256 * slot + 256)
                upper = upper + dot_tn(acts[2 * pair + slot][:, wide], grads[pair][here, :])
            lower = lower + dot_tn(hidden[pair][:, narrow], grad_mlp[pair][...])
        out[0:256, :] = upper.astype(BF)
        out[256:384, :] = lower.astype(BF)


def mlp_out_kernel(ids, *refs):
    hidden, refs = refs[:4], refs[4:]
    seeds, refs = refs[:8], refs[8:]
    pieces, refs = refs[:4], refs[4:]
    outs, (sums, w_down) = refs[:8], refs[8:]
    for place, piece in enumerate(pieces):
        w_down[rows_at(ids[ID_GPOS + place], 128), :] = piece[256:384, :]
    total = jnp.zeros((1, sums.shape[1]), F32)
    for slot in range(8):
        here = slice(256 * (slot % 2), 256 * (slot % 2) + 256)
        result = dot_nn(hidden[slot // 2][here, :], w_down[...])
        outs[slot][...] = result.astype(BF)
        total = total + jnp.sum(result * seeds[slot][...].astype(F32), axis=0, keepdims=True)
    sums[...] = jnp.concatenate([total, jnp.zeros((7, sums.shape[1]), F32)], axis=0)


def qkv_grad_kernel(ids, act, grad, packed, *refs):
    sends, keeps, held = refs[:4], refs[4:8], refs[8]
    y_here = ids[ID_Y]
    for place in range(4):
        block = ids[ID_DEST + place]
        wide = pl.ds(pl.multiple_of(block * 256, 256), 256)
        held[...] = dot_tn(act[:, wide], grad[...])
        for half, out in ((0, keeps[place]), (1, sends[place])):
            row = y_here if half == 0 else 1 - y_here
            out[:, 0:768] = held[rows_at(row, 128), :].astype(BF)
            for quarter in range(4):
                out[32 * quarter : 32 * quarter + 32, 768:1024] = packed[
                    2 * place + half, :, 256 * quarter : 256 * quarter + 256
                ]


def act_grad_kernel(grad, weight, x0, x1, x2, x3, o0, o1, o2, o3, sums):
    gain_sum = jnp.zeros((1, sums.shape[1]), F32)
    bias_sum = jnp.zeros((1, sums.shape[1]), F32)
    for slot, (frames, out) in enumerate(((x0, o0), (x1, o1), (x2, o2), (x3, o3))):
        result = dot_nt(grad[256 * slot : 256 * slot + 256, :], weight[...])
        out[...] = result.astype(BF)
        xhat, _ = normed(frames[...].astype(F32))
        gain_sum = gain_sum + jnp.sum(result * xhat, axis=0, keepdims=True)
        bias_sum = bias_sum + jnp.sum(result, axis=0, keepdims=True)
    sums[...] = jnp.concatenate(
        [gain_sum, bias_sum, jnp.zeros((6, sums.shape[1]), F32)], axis=0
    )


def last_kernel(u, v, frames, vecs, grad_resid, out):
    grad_act = u[...].astype(F32) + v[...].astype(F32)
    xhat, spread = normed(frames[...].astype(F32))
    pulled = grad_act * vecs[0:1, :]
    out[...] = grad_resid[...] + spread * (
        pulled
        - jnp.mean(pulled, axis=-1, keepdims=True)
        - xhat * jnp.mean(pulled * xhat, axis=-1, keepdims=True)
    )


def added(left, right):
    return (left.astype(F32) + right.astype(F32)).astype(BF)


def on_device(
    frames_in,
    output_grad,
    clip_kinds,
    clip_lengths,
    norm1_gain,
    norm1_bias,
    w_qkv,
    w_out,
    attn_scale,
    norm2_gain,
    norm2_bias,
    w_gate_up,
    w_down,
    mlp_scale,
    *,
    rings,
):
    depth = lax.axis_size("z")
    groups = lax.axis_size("seq")
    z_here, y_here, s_here = lax.axis_index("z"), lax.axis_index("y"), lax.axis_index("seq")
    everywhere = ("z", "y", "seq")
    plane = ("y", "seq")
    clips, slab, width = frames_in.shape
    rows = clips * slab
    device = (z_here * 2 + y_here) * groups + s_here
    devices = depth * 2 * groups
    piece_rows = w_qkv.shape[0]

    def over_seq(array_in, flip):
        return lax.ppermute(array_in, "seq", [(i, i ^ flip) for i in range(groups)])

    def over_y(array_in):
        return lax.ppermute(array_in, "y", [(0, 1), (1, 0)])

    def over_corner(array_in):
        pairs = [
            (y * groups + s, (1 - y) * groups + (s ^ 2)) for y in range(2) for s in range(groups)
        ]
        return lax.ppermute(array_in, plane, pairs)

    def over_z(array_in):
        return lax.ppermute(array_in, "z", [(i, (i + 1) % depth) for i in range(depth)])

    def gather_seq(array_in):
        near, far = over_seq(array_in, 1), over_seq(array_in, 2)
        return [array_in, near, far, over_seq(far, 1)]

    def gather_plane(array_in):
        slots = [array_in, over_seq(array_in, 1)]
        for arrived in (over_seq(array_in, 2), over_y(array_in), over_corner(array_in)):
            slots += [arrived, over_seq(arrived, 1)]
        return slots

    def scatter_plane(slots):
        sums = [added(slots[2 * p], over_seq(slots[2 * p + 1], 1)) for p in range(4)]
        return [sums[0], over_seq(sums[1], 2), over_y(sums[2]), over_corner(sums[3])]

    if rings:
        came = [(z_here - k) % depth for k in range(4)]
        dest = [(z_here - 1 - k) % depth for k in range(4)]
        pos = [came[k] * 2 + (y_here if h == 0 else 1 - y_here) for k in range(4) for h in (0, 1)]
        y_row = y_here
    else:
        came = [jnp.int32(k) for k in range(4)]
        dest = came
        pos = [jnp.int32(k) for k in range(8)]
        y_row = jnp.int32(0)
    cpos = [dest[k] * 2 + (y_row if h == 0 else 1 - y_row) for k in range(4) for h in (0, 1)]
    ids = jnp.stack([s_here, y_row, *pos, *came, *dest, *cpos]).astype(jnp.int32)

    mine = jnp.concatenate(
        [
            v.reshape(1, piece_rows)
            for v in (norm1_gain, norm1_bias, attn_scale, norm2_gain, norm2_bias, mlp_scale)
        ],
        axis=1,
    )
    if rings:
        gathered = mine
        for flip in (1, 2):
            gathered = jnp.concatenate([gathered, over_seq(gathered, flip)], axis=0)
        gathered = jnp.concatenate([gathered, over_y(gathered)], axis=0)
        for flip in (1, 2):
            other = lax.ppermute(gathered, "z", [(i, i ^ flip) for i in range(depth)])
            gathered = jnp.concatenate([gathered, other], axis=0)
        order = jnp.arange(devices)
        pick = (order[None, :] == (order[:, None] ^ device)).astype(BF)
        gathered = dot_nn(pick, gathered)
    else:
        gathered = lax.all_gather(mine, everywhere, axis=0, tiled=True).astype(F32)
    vecs = gathered.reshape(devices, 6, piece_rows).transpose(1, 0, 2).reshape(6, width)
    vecs = jnp.concatenate([vecs, jnp.zeros((2, width), F32)], axis=0)

    frame_times = s_here * slab + jnp.arange(slab)
    mask = (frame_times[None, :] < clip_lengths[:, None]).astype(F32).reshape(rows, 1)
    slot_times = (
        (jnp.arange(groups) ^ s_here)[:, None] * slab + jnp.arange(slab)[None, :]
    ).astype(F32)
    rates = 1.0 + clip_kinds.astype(F32)
    positions = slot_times[:, None, :] * rates[None, :, None]
    lane = jnp.arange(128)
    inv_freq = 10000.0 ** (-2.0 * (lane % 32).astype(F32) / HD)
    angles = positions[..., None] * inv_freq
    cosine = jnp.cos(angles)
    sine = jnp.sin(angles) * jnp.where(lane % 64 < 32, -1.0, 1.0)
    fcol = slot_times.reshape(groups * slab, 1)
    frow = slot_times.reshape(1, groups * slab)

    heads_in = w_qkv.reshape(piece_rows, 3, groups, 256).transpose(2, 0, 1, 3)
    heads_in = heads_in.reshape(groups, piece_rows, 768)
    heads_in = lax.all_to_all(heads_in, "seq", split_axis=0, concat_axis=0, tiled=True)
    heads_in = heads_in.reshape(groups * piece_rows, 768)
    units = w_down.shape[0]
    wide_in = w_gate_up.reshape(piece_rows, 2, depth, 2 * groups, units).transpose(3, 0, 1, 2, 4)
    wide_in = wide_in.reshape(2 * groups, piece_rows, 1024)
    wide_in = lax.all_to_all(wide_in, plane, split_axis=0, concat_axis=0, tiled=True)
    wide_in = wide_in.reshape(2 * groups * piece_rows, 1024)

    frames_flat = frames_in.reshape(rows, width)
    seeds_flat = output_grad.reshape(rows, width)
    frame_slots = gather_seq(frames_flat)

    if rings:
        out_in = jnp.concatenate([w_out[:, 256 * q : 256 * q + 256] for q in range(4)], axis=0)
        ring = [jnp.concatenate([heads_in, out_in], axis=1)]
        for _ in range(3):
            ring.append(over_z(ring[-1]))
        pieces = []
        for arrived in ring:
            pieces += [arrived, over_y(arrived)]
        out_pieces = jnp.stack([piece[:, 768:] for piece in pieces])
        out_slots = gather_seq(out_pieces)
        qkv_pieces = [piece[:, :768] for piece in pieces]

        first = jnp.concatenate([wide_in, w_down], axis=0)
        first, _ = lax.optimization_barrier((first, ring[3]))
        mlp_pieces = [first]
        for _ in range(3):
            mlp_pieces.append(over_z(mlp_pieces[-1]))
    else:
        full = lax.all_gather(heads_in, ("z", "y"), axis=0, tiled=True)
        qkv_pieces = [full[128 * k : 128 * k + 128] for k in range(8)]
        full = lax.all_gather(w_out, everywhere, axis=0, tiled=True)
        full = full.reshape(8, 4, 32, 4, 256)
        out_slots = [
            lax.dynamic_index_in_dim(full, s_here ^ m, 1, keepdims=False)
            .transpose(0, 2, 1, 3)
            .reshape(8, 128, 256)
            for m in range(4)
        ]
        full_in = lax.all_gather(wide_in, "z", axis=0, tiled=True)
        full_down = lax.all_gather(w_down, "z", axis=0, tiled=True)
        mlp_pieces = [
            jnp.concatenate([full_in[256 * k : 256 * k + 256], full_down[128 * k : 128 * k + 128]])
            for k in range(4)
        ]

    act_one = pl.pallas_call(
        norm_one_kernel,
        out_shape=shaped((groups, rows, width), BF),
        compiler_params=params(),
        cost_estimate=cost(16e6, 4e6),
    )(*frame_slots, vecs)
    act_four = act_one.reshape(groups, clips, slab, width)

    def by_clip(last):
        return pl.BlockSpec((groups, 1, slab, last), lambda c: (0, c, 0, 0))

    def one_clip(last):
        return pl.BlockSpec((1, slab, last), lambda c: (c, 0, 0))

    def whole(shape):
        return pl.BlockSpec(shape, lambda c: (0,) * len(shape))

    frames_all = groups * slab
    sect, weight_qkv, *mixed_sent = pl.pallas_call(
        attend_kernel,
        grid=(clips,),
        in_specs=[smem(), smem(), by_clip(width)]
        + [whole((128, 768))] * 8
        + [by_clip(128), by_clip(128), whole((frames_all, 1)), whole((1, frames_all))],
        out_specs=[by_clip(768), whole((width, 768))] + [one_clip(256)] * 4,
        out_shape=[shaped((groups, clips, slab, 768), BF), shaped((width, 768), BF)]
        + [shaped((clips, slab, 256), BF)] * 4,
        compiler_params=params(),
        cost_estimate=cost(2.4e9, 8e6),
    )(ids, clip_lengths, act_four, *qkv_pieces, cosine, sine, fcol, frow)
    mixed = [m.reshape(rows, 256) for m in mixed_sent]
    mixed = [mixed[0]] + [over_seq(mixed[m], m) for m in range(1, 4)]

    weight_out, attn_out, resid, act_two = pl.pallas_call(
        middle_kernel,
        in_specs=[smem()] + [vmem()] * 11,
        out_shape=[
            shaped((width, width), BF),
            shaped((rows, width), F32),
            shaped((rows, width), F32),
            shaped((rows, width), BF),
        ],
        compiler_params=params(),
        cost_estimate=cost(0.6e9, 9e6),
    )(ids, *mixed, *out_slots, frames_flat, mask, vecs)

    seeds_masked = (seeds_flat.astype(F32) * mask).astype(BF)
    seed_slots = gather_plane(seeds_masked)
    act_slots = gather_plane(act_two)
    hidden_width = FF // (2 * groups)
    pair_out = [None] * 4
    for pair in (3, 1, 2, 0):
        pair_out[pair] = pl.pallas_call(
            mlp_kernel,
            in_specs=[smem()] + [vmem()] * 9,
            out_shape=[
                shaped((2 * rows, hidden_width), BF),
                shaped((2 * rows, 2 * hidden_width), BF),
                shaped((2 * rows, width), BF),
                shaped((rows, width), BF),
                shaped((rows, width), BF),
            ],
            scratch_shapes=[
                pltpu.VMEM((width, 2 * hidden_width), BF),
                pltpu.VMEM((hidden_width, width), BF),
            ],
            compiler_params=params(),
            cost_estimate=cost(3.2e9, 10e6),
        )(
            ids,
            act_slots[2 * pair],
            act_slots[2 * pair + 1],
            seed_slots[2 * pair],
            seed_slots[2 * pair + 1],
            *mlp_pieces,
            vecs,
        )
    hidden = [p[0] for p in pair_out]
    grads = [p[1] for p in pair_out]
    grad_mlp = [p[2] for p in pair_out]
    back_slots = [half for p in pair_out for half in p[3:]]
    back_parts = scatter_plane(back_slots)

    mlp_grads = []
    for places in ((0,), (1, 2, 3)):
        mlp_grads += pl.pallas_call(
            functools.partial(mlp_grad_kernel, places),
            in_specs=[smem()] + [vmem()] * 20,
            out_shape=[shaped((384, width), BF)] * len(places),
            compiler_params=params(),
            cost_estimate=cost(1.6e9 * len(places), 14e6),
        )(ids, *act_slots, *grads, *hidden, *grad_mlp)

    *out_parts, scale_sums = pl.pallas_call(
        mlp_out_kernel,
        in_specs=[smem()] + [vmem()] * 16,
        out_shape=[shaped((rows, width), BF)] * 8 + [shaped((8, width), F32)],
        scratch_shapes=[pltpu.VMEM((hidden_width, width), BF)],
        compiler_params=params(),
        cost_estimate=cost(2.2e9, 11e6),
    )(ids, *hidden, *seed_slots, *mlp_pieces)

    grad_resid, grad_attn, g0, g1, g2, g3, middle_sums = pl.pallas_call(
        middle_back_kernel,
        in_specs=[smem()] + [vmem()] * 10,
        out_shape=[shaped((rows, width), F32), shaped((rows, width), BF)]
        + [shaped((rows, 256), BF)] * 4
        + [shaped((8, width), F32)],
        compiler_params=params(),
        cost_estimate=cost(0.6e9, 9e6),
    )(ids, *back_parts, resid, attn_out, seeds_flat, mask, vecs, weight_out)
    mixed_grads = [g0] + [over_seq(g, m) for m, g in ((1, g1), (2, g2), (3, g3))]
    mixed_grads = [g.reshape(clips, slab, 256) for g in mixed_grads]

    out_grads = pl.pallas_call(
        out_grad_kernel,
        in_specs=[smem()] + [vmem()] * 5,
        out_shape=[shaped((8, 32, width), BF)] * 4,
        scratch_shapes=[pltpu.VMEM((width, width), BF)],
        compiler_params=params(),
        cost_estimate=cost(0.6e9, 4e6),
    )(ids, *mixed, grad_attn)
    if rings:
        packed = added(
            added(out_grads[0], over_seq(out_grads[1], 1)),
            over_seq(added(out_grads[2], over_seq(out_grads[3], 1)), 2),
        )
    else:
        packed = out_grads[0]

    grad_proj = pl.pallas_call(
        attend_back_kernel,
        grid=(clips,),
        in_specs=[smem(), by_clip(768)]
        + [one_clip(256)] * 4
        + [by_clip(128), by_clip(128), whole((frames_all, 1)), whole((1, frames_all))],
        out_specs=by_clip(768),
        out_shape=shaped((groups, clips, slab, 768), BF),
        compiler_params=params(),
        cost_estimate=cost(2.0e9, 5e6),
    )(clip_lengths, sect, *mixed_grads, cosine, sine, fcol, frow)
    grad_proj = grad_proj.reshape(groups * rows, 768)

    qkv_out = pl.pallas_call(
        qkv_grad_kernel,
        in_specs=[smem()] + [vmem()] * 3,
        out_shape=[shaped((128, 1024), BF)] * 8,
        scratch_shapes=[pltpu.VMEM((256, 768), F32)],
        compiler_params=params(),
        cost_estimate=cost(1.6e9, 6e6),
    )(ids, act_one.reshape(groups * rows, width), grad_proj, packed)
    sends, keeps = qkv_out[:4], qkv_out[4:]

    *act_parts, norm_sums = pl.pallas_call(
        act_grad_kernel,
        out_shape=[shaped((rows, width), BF)] * 4 + [shaped((8, width), F32)],
        compiler_params=params(),
        cost_estimate=cost(1.6e9, 7e6),
    )(grad_proj, weight_qkv, *frame_slots)
    near = added(act_parts[0], over_seq(act_parts[1], 1))
    far = over_seq(added(act_parts[2], over_seq(act_parts[3], 1)), 2)
    input_grad = pl.pallas_call(
        last_kernel,
        out_shape=shaped((rows, width), F32),
        compiler_params=params(),
        cost_estimate=cost(8e6, 4e6),
    )(near, far, frames_flat, vecs, grad_resid).reshape(frames_in.shape)

    out_parts = scatter_plane(out_parts)
    mlp_out = sum(part.astype(F32) for part in out_parts)
    layer_out = (resid + mask * vecs[5:6, :] * mlp_out).astype(BF).reshape(frames_in.shape)

    sums = jnp.concatenate([norm_sums[0:2], middle_sums[0:3], scale_sums[0:1]], axis=0)
    sums = jnp.concatenate([sums, jnp.zeros((2, width), F32)], axis=0)
    if rings:
        for flip in (1, 2):
            sums = sums + over_seq(sums, flip)
        sums = sums + over_y(sums)
        for flip in (1, 2):
            sums = sums + lax.ppermute(sums, "z", [(i, i ^ flip) for i in range(depth)])
        total = mlp_grads[0]
        for place in range(1, 4):
            total = over_z(total).astype(F32) + mlp_grads[place].astype(F32)
            total = total.astype(BF) if place < 3 else total
        sum_in, sum_down = total[:256].astype(BF), total[256:]

        parts = [added(keeps[k], over_y(sends[k])) for k in range(4)]
        total = parts[0]
        for place in range(1, 4):
            total = over_z(total).astype(F32) + parts[place].astype(F32)
            total = total.astype(BF) if place < 3 else total
        sum_qkv = total[:, :768].astype(BF)
        sum_out = jnp.concatenate(
            [total[piece_rows * q : piece_rows * (q + 1), 768:] for q in range(4)], axis=1
        )
    else:
        sums = lax.psum(sums, everywhere)
        full = jnp.concatenate([block[:256] for block in mlp_grads])
        sum_in = lax.psum_scatter(full, "z", scatter_dimension=0, tiled=True)
        full = jnp.concatenate([block[256:] for block in mlp_grads])
        sum_down = lax.psum_scatter(full, "z", scatter_dimension=0, tiled=True).astype(F32)
        full = jnp.concatenate([p[:, :768] for k in range(4) for p in (keeps[k], sends[k])])
        sum_qkv = lax.psum_scatter(full, ("z", "y"), scatter_dimension=0, tiled=True)
        full = jnp.stack(out_grads)
        full = jnp.stack(
            [lax.dynamic_index_in_dim(full, s_here ^ m, 0, keepdims=False) for m in range(4)], axis=1
        ).reshape(width, width)
        sum_out = lax.psum_scatter(full, everywhere, scatter_dimension=0, tiled=True).astype(F32)
    sums = lax.dynamic_index_in_dim(
        sums.reshape(8, devices, piece_rows), device, 1, keepdims=False
    )

    wide_out = sum_in.reshape(2 * groups, piece_rows, 1024)
    wide_out = lax.all_to_all(wide_out, plane, split_axis=0, concat_axis=0, tiled=True)
    wide_out = wide_out.reshape(2 * groups, piece_rows, 2, depth, units).transpose(1, 2, 3, 0, 4)
    sum_gate_up = wide_out.reshape(w_gate_up.shape).astype(F32)
    heads_out = sum_qkv.reshape(groups, piece_rows, 768)
    heads_out = lax.all_to_all(heads_out, "seq", split_axis=0, concat_axis=0, tiled=True)
    heads_out = heads_out.reshape(groups, piece_rows, 3, 256).transpose(1, 2, 0, 3)
    sum_qkv = heads_out.reshape(w_qkv.shape).astype(F32)

    return (
        layer_out,
        input_grad,
        sums[0],
        sums[1],
        sum_qkv,
        sum_out,
        sums[4],
        sums[2],
        sums[3],
        sum_gate_up,
        sum_down,
        sums[5],
    )


def solution(mesh):
    clip_groups, groups = mesh.shape["clips"], mesh.shape["seq"]
    depth = clip_groups // 2
    split = Mesh(mesh.devices.reshape(depth, 2, groups), ("z", "y", "seq"))
    clips, everywhere = ("z", "y"), ("z", "y", "seq")
    by_frame, by_clip = P(clips, "seq", None), P(clips)
    by_row, by_entry = P(everywhere, None), P(everywhere)
    return jax.shard_map(
        functools.partial(on_device, rings=depth == 4 and groups == 4),
        mesh=split,
        in_specs=(
            by_frame, by_frame, by_clip, by_clip, by_entry, by_entry, by_row, by_row,
            by_entry, by_entry, by_entry, by_row, by_row, by_entry,
        ),
        out_specs=(
            by_frame, by_frame, by_entry, by_entry, by_row, by_row, by_entry, by_entry,
            by_entry, by_row, by_row, by_entry,
        ),
        check_vma=False,
    )
```

```python
import functools

import jax
import jax.numpy as jnp
import numpy as np
from jax import lax
from jax.experimental import pallas as pl
from jax.experimental.pallas import tpu as pltpu
from jax.sharding import Mesh
from jax.sharding import PartitionSpec as P

H = 16
HD = 64
FF = 4096
WIN = 128
NEG_FILL = -1000000000.0
EPS = 1e-05
BF = jnp.bfloat16
F32 = jnp.float32
VMEM_BYTES = 56 * 1024 * 1024
COST_SCALE = (10, 10, 10, 10)
STAGES = ()

ID_SEQ, ID_Y, ID_POS, ID_DEST, ID_CPOS = 0, 1, 2, 10, 14


def dot_nn(left, right):
    return jnp.dot(left, right, preferred_element_type=F32)


def dot_nt(left, right):
    return lax.dot_general(left, right, (((1,), (1,)), ((), ())), preferred_element_type=F32)


def dot_tn(left, right):
    return lax.dot_general(left, right, (((0,), (0,)), ((), ())), preferred_element_type=F32)


def smem():
    return pl.BlockSpec(memory_space=pltpu.SMEM)


def vmem():
    return pl.BlockSpec(memory_space=pltpu.VMEM)


def shaped(shape, dtype):
    return jax.ShapeDtypeStruct(shape, dtype)


def params():
    return pltpu.CompilerParams(vmem_limit_bytes=VMEM_BYTES)


def cost(phase, flops, moved):
    scale = COST_SCALE[phase]
    return pl.CostEstimate(
        flops=int(flops * scale), bytes_accessed=int(moved * scale), transcendentals=0
    )


def rows_at(index, size):
    return pl.ds(pl.multiple_of(index * size, size), size)


def normed(values):
    center = values - jnp.mean(values, axis=-1, keepdims=True)
    spread = lax.rsqrt(jnp.mean(center * center, axis=-1, keepdims=True) + EPS)
    return center * spread, spread


def pack_kernel(ids, weight, vector, *outs):
    me = ids[ID_SEQ]
    for slot, out in enumerate(outs):
        other = jnp.bitwise_xor(me, slot)
        for part in range(3):
            start = pl.multiple_of(part * 1024 + other * 256, 256)
            out[0:32, 256 * part : 256 * part + 256] = weight[:, pl.ds(start, 256)]
        out[32:48, 0:128] = vector[...]
        out[32:48, 128:768] = jnp.zeros((16, 640), BF)


def packet_kernel(s0, s1, s2, s3, packet):
    total = jnp.zeros((16, 128), F32)
    for slot, ref in enumerate((s0, s1, s2, s3)):
        packet[32 * slot : 32 * slot + 32, :] = ref[0:32, :]
        total = total + ref[32:48, 0:128].astype(F32)
    packet[128:144, 0:128] = total.astype(BF)
    packet[128:144, 128:768] = jnp.zeros((16, 640), BF)


def unpack_kernel(ids, *refs):
    pieces, (weight, vecs) = refs[:8], refs[8:]
    me = ids[ID_SEQ]
    for place, piece in enumerate(pieces):
        spot = ids[ID_POS + place]
        for slot in range(4):
            start = pl.multiple_of(spot * 128 + jnp.bitwise_xor(me, slot) * 32, 32)
            weight[pl.ds(start, 32), :] = piece[32 * slot : 32 * slot + 32, :]
        lanes = pl.ds(pl.multiple_of(spot * 128, 128), 128)
        vecs[:, lanes] = piece[128:144, 0:128].astype(F32)[0:8, :]


def norm_stats_kernel(x0, x1, x2, x3, mean, spread):
    for slot, frames in enumerate((x0, x1, x2, x3)):
        values = frames[...].astype(F32)
        middle = jnp.mean(values, axis=-1, keepdims=True)
        center = values - middle
        mean[slot] = middle
        spread[slot] = lax.rsqrt(jnp.mean(center * center, axis=-1, keepdims=True) + EPS)


def visible_bias(fcol, frow, length):
    gap = jnp.abs(fcol[...] - frow[...])
    seen = (gap <= WIN // 2) & (frow[...] < length.astype(F32))
    return jnp.where(seen, 0.0, NEG_FILL)


def turn(values, cosine, sine, lower):
    swapped = jnp.where(lower, pltpu.roll(values, 96, 1), pltpu.roll(values, 32, 1))
    return values * cosine + swapped * sine


def lane_masks():
    lane = lax.broadcasted_iota(jnp.int32, (1, 128), 1)
    lower = lane % 64 < 32
    return lower, [(lane // 64 == half).astype(F32) for half in (0, 1)]


def attend_kernel(
    lens, x0, x1, x2, x3, mean, spread, weight, vecs, cosine, sine, fcol, frow,
    sect, act, m0, m1, m2, m3,
):
    clip = pl.program_id(0)
    slab, width = x0.shape[1:]
    rows = 4 * slab
    frames = jnp.concatenate([x[0] for x in (x0, x1, x2, x3)], axis=0).astype(F32)
    frames = (frames - mean[...].reshape(rows, 1)) * spread[...].reshape(rows, 1)
    normal = (frames * vecs[0:1, :] + vecs[1:2, :]).astype(BF)
    act[...] = normal.reshape(act.shape)
    projected = dot_nn(normal, weight[...])
    cos_rows = cosine[...].reshape(rows, 128)
    sin_rows = sine[...].reshape(rows, 128)
    lower, masks = lane_masks()
    lower = jnp.broadcast_to(lower, (rows, 128))
    chunks = []
    for place in range(6):
        chunk = projected[:, 128 * place : 128 * place + 128]
        if place < 4:
            chunk = turn(chunk, cos_rows, sin_rows, lower)
        chunk = chunk.astype(BF)
        chunks.append(chunk)
        sect[:, 0, :, 128 * place : 128 * place + 128] = chunk.reshape(-1, slab, 128)
    bias = visible_bias(fcol, frow, lens[clip])
    for pair in range(2):
        total = jnp.zeros((rows, 128), F32)
        for half in range(2):
            mask = masks[half].astype(BF)
            scores = dot_nt(chunks[pair] * mask, chunks[2 + pair]) * HD ** (-0.5) + bias
            expo = jnp.exp(scores - jnp.max(scores, axis=-1, keepdims=True))
            weights = (expo * (1.0 / jnp.sum(expo, axis=-1, keepdims=True))).astype(BF)
            total = total + dot_nn(weights, chunks[4 + pair] * mask)
        total = total.astype(BF)
        for slot, out in enumerate((m0, m1, m2, m3)):
            out[0, :, 128 * pair : 128 * pair + 128] = total[slab * slot : slab * (slot + 1)]


def attend_back_kernel(lens, sect, g0, g1, g2, g3, cosine, sine, fcol, frow, grad):
    clip = pl.program_id(0)
    slab = sect.shape[2]
    rows = sect.shape[0] * slab
    cos_rows = cosine[...].reshape(rows, 128)
    sin_rows = -sine[...].reshape(rows, 128)
    lower, masks = lane_masks()
    lower = jnp.broadcast_to(lower, (rows, 128))
    bias = visible_bias(fcol, frow, lens[clip])

    def part(place):
        return sect[:, 0, :, 128 * place : 128 * place + 128].reshape(rows, 128)

    def put(place, values):
        grad[:, 0, :, 128 * place : 128 * place + 128] = values.astype(BF).reshape(-1, slab, 128)

    for pair in range(2):
        queries, keys_in, values_in = part(pair), part(2 + pair), part(4 + pair)
        mixed_grad = jnp.concatenate(
            [g[0, :, 128 * pair : 128 * pair + 128] for g in (g0, g1, g2, g3)], axis=0
        )
        grad_q = jnp.zeros((rows, 128), F32)
        grad_k = jnp.zeros((rows, 128), F32)
        grad_v = jnp.zeros((rows, 128), F32)
        for half in range(2):
            mask = masks[half].astype(BF)
            query = queries * mask
            upper = mixed_grad * mask
            scores = dot_nt(query, keys_in) * HD ** (-0.5) + bias
            expo = jnp.exp(scores - jnp.max(scores, axis=-1, keepdims=True))
            probs = expo * (1.0 / jnp.sum(expo, axis=-1, keepdims=True))
            grad_v = grad_v + dot_tn(probs.astype(BF), upper)
            grad_probs = dot_nt(upper, values_in)
            centre = jnp.sum(probs * grad_probs, axis=-1, keepdims=True)
            grad_scores = (probs * (grad_probs - centre)).astype(BF)
            grad_q = grad_q + dot_nn(grad_scores, keys_in * mask)
            grad_k = grad_k + dot_tn(grad_scores, query)
        grad_q = (grad_q * HD ** (-0.5)).astype(BF).astype(F32)
        grad_k = (grad_k * HD ** (-0.5)).astype(BF).astype(F32)
        put(pair, turn(grad_q, cos_rows, sin_rows, lower))
        put(2 + pair, turn(grad_k, cos_rows, sin_rows, lower))
        put(4 + pair, grad_v)


def middle_kernel(
    ids, m0, m1, m2, m3, w0, w1, w2, w3, frames, mask, vecs, weight, attn_out, resid, act
):
    me = ids[ID_SEQ]
    for slot, packed in enumerate((w0, w1, w2, w3)):
        other = jnp.bitwise_xor(me, slot)
        for place in range(8):
            start = pl.multiple_of(ids[ID_POS + place] * 128 + other * 32, 32)
            weight[pl.ds(start, 32), :] = packed[place]
    total = jnp.zeros(attn_out.shape, F32)
    for slot, mixed in enumerate((m0, m1, m2, m3)):
        block = weight[rows_at(jnp.bitwise_xor(me, slot), 256), :]
        total = total + dot_nn(mixed[...], block)
    attn_out[...] = total
    summed = frames[...].astype(F32) + mask[...] * vecs[2:3, :] * total
    resid[...] = summed
    xhat, _ = normed(summed)
    act[...] = (xhat * vecs[3:4, :] + vecs[4:5, :]).astype(BF)


def middle_back_kernel(
    ids, q0, q1, q2, q3, resid, attn_out, grad_in, mask, vecs, weight,
    grad_resid, grad_attn, g0, g1, g2, g3, sums,
):
    me = ids[ID_SEQ]
    grad_act = q0[...].astype(F32) + q1[...].astype(F32) + q2[...].astype(F32) + q3[...].astype(F32)
    xhat, spread = normed(resid[...])
    sums[0:1, :] = jnp.sum(grad_act * xhat, axis=0, keepdims=True)
    sums[1:2, :] = jnp.sum(grad_act, axis=0, keepdims=True)
    pulled = grad_act * vecs[3:4, :]
    pulled = spread * (
        pulled
        - jnp.mean(pulled, axis=-1, keepdims=True)
        - xhat * jnp.mean(pulled * xhat, axis=-1, keepdims=True)
    )
    total = grad_in[...].astype(F32) + pulled
    grad_resid[...] = total
    masked = mask[...] * total
    sums[2:3, :] = jnp.sum(masked * attn_out[...], axis=0, keepdims=True)
    sums[3:8, :] = jnp.zeros((5, sums.shape[1]), F32)
    scaled = (masked * vecs[2:3, :]).astype(BF)
    grad_attn[...] = scaled
    for slot, out in enumerate((g0, g1, g2, g3)):
        block = weight[rows_at(jnp.bitwise_xor(me, slot), 256), :]
        out[...] = dot_nt(scaled, block).astype(BF)


def out_grad_kernel(ids, m0, m1, m2, m3, grad_attn, even, odd, held):
    me = ids[ID_SEQ]
    for slot, mixed in enumerate((m0, m1, m2, m3)):
        held[rows_at(jnp.bitwise_xor(me, slot), 256), :] = dot_tn(mixed[...], grad_attn[...]).astype(
            BF
        )
    for slot in range(4):
        other = jnp.bitwise_xor(me, slot)
        out = odd if slot % 2 else even
        for place in range(8):
            start = pl.multiple_of(ids[ID_CPOS + place] * 128 + other * 32, 32)
            out[slot // 2, place] = held[pl.ds(start, 32), :]


def piece_parts(depth, held, place):
    wide, down = 1024 // depth, held // depth
    start = (wide + down) * place
    return (
        (slice(start, start + wide), slice(wide * place, wide * place + wide)),
        (slice(start + wide, start + wide + down), slice(down * place, down * place + down)),
    )


def spread_pieces(depth, pieces, w_in, w_down):
    for place in range(depth):
        upper, lower = piece_parts(depth, w_down.shape[0], place)
        if w_in is not None:
            w_in[upper[1], :] = pieces[upper[0], :]
        w_down[lower[1], :] = pieces[lower[0], :]


def mlp_kernel(
    depth, a0, a1, o0, o1, pieces, vecs, hidden, grads, grad_mlp, even, odd, w_in, w_down
):
    spread_pieces(depth, pieces, w_in, w_down)
    width = hidden.shape[1]
    for slot, (act, seed, out) in enumerate(((a0, o0, even), (a1, o1, odd))):
        here = slice(256 * slot, 256 * slot + 256)
        gate_up = dot_nn(act[...], w_in[...])
        gate, up = gate_up[:, :width], gate_up[:, width:]
        pulled = (vecs[5:6, :] * seed[...].astype(F32)).astype(BF)
        grad_mlp[here, :] = pulled
        grad_hidden = dot_nt(pulled, w_down[...])
        sig = jax.nn.sigmoid(gate)
        silu = gate * sig
        hidden[here, :] = (silu * up).astype(BF)
        grad_gate = grad_hidden * up * sig * (1.0 + gate * (1.0 - sig))
        grads[here, :width] = grad_gate.astype(BF)
        grads[here, width:] = (grad_hidden * silu).astype(BF)
        out[...] = dot_nt(grads[here, :], w_in[...]).astype(BF)


def mlp_grad_kernel(depth, *refs):
    acts, refs = refs[:8], refs[8:]
    grads, refs = refs[:4], refs[4:]
    hidden, refs = refs[:4], refs[4:]
    grad_mlp, (out, upper, lower) = refs[:4], refs[4:]
    for block in range(4):
        wide = slice(256 * block, 256 * block + 256)
        narrow = slice(128 * block, 128 * block + 128)
        total = jnp.zeros((256, out.shape[1]), F32)
        rest = jnp.zeros((128, out.shape[1]), F32)
        for pair in range(4):
            for slot in range(2):
                here = slice(256 * slot, 256 * slot + 256)
                total = total + dot_tn(acts[2 * pair + slot][:, wide], grads[pair][here, :])
            rest = rest + dot_tn(hidden[pair][:, narrow], grad_mlp[pair][...])
        upper[wide, :] = total.astype(BF)
        lower[narrow, :] = rest.astype(BF)
    for place in range(depth):
        first, second = piece_parts(depth, lower.shape[0], place)
        out[first[0], :] = upper[first[1], :]
        out[second[0], :] = lower[second[1], :]


def mlp_out_kernel(depth, *refs):
    hidden, refs = refs[:4], refs[4:]
    seeds, refs = refs[:8], refs[8:]
    pieces, refs = refs[0], refs[1:]
    even, odd, sums, w_down = refs
    spread_pieces(depth, pieces, None, w_down)
    total = jnp.zeros((1, sums.shape[1]), F32)
    for slot in range(8):
        here = slice(256 * (slot % 2), 256 * (slot % 2) + 256)
        result = dot_nn(hidden[slot // 2][here, :], w_down[...])
        out = odd if slot % 2 else even
        out[slot // 2] = result.astype(BF)
        total = total + jnp.sum(result * seeds[slot][...].astype(F32), axis=0, keepdims=True)
    sums[...] = jnp.concatenate([total, jnp.zeros((7, sums.shape[1]), F32)], axis=0)


def qkv_grad_kernel(
    ids, act, grad, packed, norm_sums, middle_sums, scale_sums, send_first, send_two, send_last, keep, held, sums
):
    sums[0:8, :] = jnp.concatenate(
        [norm_sums[0:2, :], middle_sums[0:3, :], scale_sums[0:1, :], jnp.zeros((2, 1024), F32)],
        axis=0,
    )
    sums[8:16, :] = jnp.zeros((8, 1024), F32)
    y_here = ids[ID_Y]
    for place in range(4):
        block = ids[ID_DEST + place]
        wide = pl.ds(pl.multiple_of(block * 256, 256), 256)
        held[...] = dot_tn(act[:, wide], grad[...])
        send = (send_first, send_two.at[0], send_two.at[1], send_last)[place]
        for half, out in ((0, keep.at[place]), (1, send)):
            row = y_here if half == 0 else 1 - y_here
            out[0:128, 0:768] = held[rows_at(row, 128), :].astype(BF)
            for quarter in range(4):
                out[32 * quarter : 32 * quarter + 32, 768:1024] = packed[
                    2 * place + half, :, 256 * quarter : 256 * quarter + 256
                ]
            lanes = pl.ds(pl.multiple_of(block * 256 + row * 128, 128), 128)
            out[128:144, 0:128] = sums[:, lanes].astype(BF)
            out[128:144, 128:1024] = jnp.zeros((16, 896), BF)


def prepare_kernel(total, parts):
    for place in range(4):
        parts[place, 0:32, :] = total[32 * place : 32 * place + 32, 0:768].astype(BF)
        block = total[128:144, 0:128]
        block = pltpu.roll(block, 128 - 32 * place, 1) if place else block
        parts[place, 32:48, 0:128] = block.astype(BF)
        parts[place, 32:48, 128:768] = jnp.zeros((16, 640), BF)


def finish_kernel(parts, out, sums):
    total = jnp.zeros((16, 128), F32)
    for place in range(4):
        for part in range(3):
            start = 1024 * part + 256 * place
            here = 256 * part
            out[:, start : start + 256] = parts[place, 0:32, here : here + 256].astype(F32)
        total = total + parts[place, 32:48, 0:128].astype(F32)
    sums[...] = total[0:8, :]


def act_grad_kernel(grad, weight, x0, x1, x2, x3, even, odd, sums):
    gain_sum = jnp.zeros((1, sums.shape[1]), F32)
    bias_sum = jnp.zeros((1, sums.shape[1]), F32)
    for slot, frames in enumerate((x0, x1, x2, x3)):
        result = dot_nt(grad[256 * slot : 256 * slot + 256, :], weight[...])
        out = odd if slot % 2 else even
        out[slot // 2] = result.astype(BF)
        xhat, _ = normed(frames[...].astype(F32))
        gain_sum = gain_sum + jnp.sum(result * xhat, axis=0, keepdims=True)
        bias_sum = bias_sum + jnp.sum(result, axis=0, keepdims=True)
    sums[...] = jnp.concatenate(
        [gain_sum, bias_sum, jnp.zeros((6, sums.shape[1]), F32)], axis=0
    )


def last_kernel(u, v, frames, vecs, grad_resid, out):
    grad_act = u[...].astype(F32) + v[...].astype(F32)
    xhat, spread = normed(frames[...].astype(F32))
    pulled = grad_act * vecs[0:1, :]
    out[...] = grad_resid[...] + spread * (
        pulled
        - jnp.mean(pulled, axis=-1, keepdims=True)
        - xhat * jnp.mean(pulled * xhat, axis=-1, keepdims=True)
    )


def added(left, right):
    return (left.astype(F32) + right.astype(F32)).astype(BF)


def after(value, *first):
    return lax.optimization_barrier((value, first))[0]


def stage(always, steps, *values):
    if steps.__name__ not in STAGES:
        return steps(*values)
    made = jax.eval_shape(steps, *values)

    def none(*values):
        return jax.tree.map(lambda leaf: jnp.zeros(leaf.shape, leaf.dtype), made)

    return lax.cond(always, steps, none, *values)


def on_device(
    frames_in,
    output_grad,
    clip_kinds,
    clip_lengths,
    norm1_gain,
    norm1_bias,
    w_qkv,
    w_out,
    attn_scale,
    norm2_gain,
    norm2_bias,
    w_gate_up,
    w_down,
    mlp_scale,
    *,
    rings,
):
    depth = lax.axis_size("z")
    groups = lax.axis_size("seq")
    z_here, y_here, s_here = lax.axis_index("z"), lax.axis_index("y"), lax.axis_index("seq")
    everywhere = ("z", "y", "seq")
    plane = ("y", "seq")
    clips, slab, width = frames_in.shape
    rows = clips * slab
    device = (z_here * 2 + y_here) * groups + s_here
    devices = depth * 2 * groups
    piece_rows = w_qkv.shape[0]

    def over_seq(array_in, flip):
        return lax.ppermute(array_in, "seq", [(i, i ^ flip) for i in range(groups)])

    def over_y(array_in):
        return lax.ppermute(array_in, "y", [(0, 1), (1, 0)])

    def over_corner(array_in):
        pairs = [
            (y * groups + s, (1 - y) * groups + (s ^ 2)) for y in range(2) for s in range(groups)
        ]
        return lax.ppermute(array_in, plane, pairs)

    def over_z(array_in, step):
        return lax.ppermute(array_in, "z", [(i, (i + step) % depth) for i in range(depth)])

    def gather_z(array_in):
        left, right = over_z(array_in, 1), over_z(array_in, -1)
        return [array_in, left, right, over_z(left, 1)]

    def scatter_z(blocks):
        passed = added(blocks[1], over_z(blocks[0], 1))
        left, right = over_z(passed, 1), over_z(blocks[2], -1)
        return blocks[3].astype(F32) + left.astype(F32) + right.astype(F32)

    def gather_seq(array_in):
        near, far = over_seq(array_in, 1), over_seq(array_in, 2)
        return [array_in, near, far, over_seq(far, 1)]

    def gather_plane(array_in):
        slots = [array_in, over_seq(array_in, 1)]
        for arrived in (over_seq(array_in, 2), over_y(array_in), over_corner(array_in)):
            slots += [arrived, over_seq(arrived, 1)]
        return slots

    def scatter_plane(slots):
        return send_plane(
            [added(slots[2 * p], over_seq(slots[2 * p + 1], 1)) for p in range(4)]
        )

    def send_plane(sums):
        return [sums[0], over_seq(sums[1], 2), over_y(sums[2]), over_corner(sums[3])]

    def exchange_plane(array_in):
        parts = lax.all_to_all(array_in, plane, split_axis=0, concat_axis=0, tiled=True)
        return parts.reshape(-1, array_in.shape[-1])

    def norm_stats(slots):
        return pl.pallas_call(
            norm_stats_kernel,
            name="norm_stats",
            out_shape=[shaped((groups, rows, 1), F32)] * 2,
            compiler_params=params(),
            cost_estimate=cost(0, 16e6, 6e6),
        )(*slots)

    if rings:
        came = [(z_here + k) % depth for k in (0, -1, 1, -2)]
        dest = [(z_here + k) % depth for k in (2, 1, -1, 0)]
        pos = [came[k] * 2 + (y_here if h == 0 else 1 - y_here) for k in range(4) for h in (0, 1)]
        y_row = y_here
    else:
        dest = [jnp.int32(k) for k in range(4)]
        pos = [jnp.int32(k) for k in range(8)]
        y_row = jnp.int32(0)
    cpos = [dest[k] * 2 + (y_row if h == 0 else 1 - y_row) for k in range(4) for h in (0, 1)]
    ids = jnp.stack([s_here, y_row, *pos, *dest, *cpos]).astype(jnp.int32)

    frame_times = s_here * slab + jnp.arange(slab)
    mask = (frame_times[None, :] < clip_lengths[:, None]).astype(F32).reshape(rows, 1)
    slot_times = (
        (jnp.arange(groups) ^ s_here)[:, None] * slab + jnp.arange(slab)[None, :]
    ).astype(F32)
    rates = 1.0 + clip_kinds.astype(F32)
    positions = slot_times[:, None, :] * rates[None, :, None]
    lane = jnp.arange(128)
    inv_freq = 10000.0 ** (-2.0 * (lane % 32).astype(F32) / HD)
    angles = positions[..., None] * inv_freq
    cosine = jnp.cos(angles)
    sine = jnp.sin(angles) * jnp.where(lane % 64 < 32, -1.0, 1.0)
    fcol = slot_times.reshape(groups * slab, 1)
    frow = slot_times.reshape(1, groups * slab)

    frames_flat = frames_in.reshape(rows, width)
    seeds_flat = output_grad.reshape(rows, width)
    seeds_masked = (seeds_flat.astype(F32) * mask).astype(BF)
    vectors = (norm1_gain, norm1_bias, attn_scale, norm2_gain, norm2_bias, mlp_scale)
    units = w_down.shape[0]
    hidden_width = FF // (2 * groups)
    frames_all = groups * slab
    wide_in = w_gate_up.reshape(piece_rows, 2, depth, 2 * groups, units).transpose(3, 0, 1, 2, 4)
    wide_in = wide_in.reshape(2 * groups, piece_rows, 1024)
    run = functools.partial(stage, clip_lengths[0] > 0)

    def by_clip(last):
        return pl.BlockSpec((groups, 1, slab, last), lambda c: (0, c, 0, 0))

    def one_clip(last):
        return pl.BlockSpec((1, slab, last), lambda c: (c, 0, 0))

    def whole(shape):
        return pl.BlockSpec(shape, lambda c: (0,) * len(shape))

    def begin():
        mine = jnp.pad(jnp.stack(vectors), ((0, 10), (0, 96)))
        mine = jnp.roll(mine, s_here * 32, axis=1)
        slots = pl.pallas_call(
            pack_kernel,
            name="pack",
            in_specs=[smem(), vmem(), vmem()],
            out_shape=[shaped((48, 768), BF)] * 4,
            compiler_params=params(),
            cost_estimate=cost(0, 1e6, 5e5),
        )(ids, w_qkv, mine)
        slots = [slots[0]] + [over_seq(slots[m], m) for m in (2, 3, 1)]
        packet = pl.pallas_call(
            packet_kernel,
            name="packet",
            out_shape=shaped((144, 768), BF),
            compiler_params=params(),
            cost_estimate=cost(0, 1e6, 8e5),
        )(*after((slots[0], slots[3], slots[1], slots[2]), cosine, sine, fcol, frow))
        return packet

    def to_neighbours(packet):
        wide = exchange_plane(wide_in)
        return (
            over_z(packet, 1),
            over_z(packet, -1),
            over_y(packet),
            over_seq(frames_flat, 2),
            over_seq(frames_flat, 1),
            jnp.concatenate([wide, w_down], axis=0),
        )

    def further(left, right, frame_x, frame_near):
        frame_last = over_seq(frame_x, 1)
        return (
            over_z(left, 1),
            over_y(left),
            over_y(right),
            over_seq(seeds_masked, 2),
            over_z(w_out, 1),
            over_z(w_out, -1),
            frame_last,
            norm_stats([frames_flat, frame_near, frame_x, frame_last]),
        )

    def unpack(pieces, out):
        last_y = over_y(pieces[-1])
        out_last = over_z(out, 1)
        weight_qkv, vecs = pl.pallas_call(
            unpack_kernel,
            name="unpack",
            in_specs=[smem()] + [vmem()] * 8,
            out_shape=[shaped((width, 768), BF), shaped((8, width), F32)],
            compiler_params=params(),
            cost_estimate=cost(1, 1e6, 4e6),
        )(ids, *pieces, last_y)
        return weight_qkv, vecs, out_last

    def attend(frame_slots, stats, weight_qkv, vecs):
        frame_slots = [slot.reshape(clips, slab, width) for slot in frame_slots]
        stats = [stat.reshape(groups, clips, slab, 1) for stat in stats]
        sect, act_one, *mixed = pl.pallas_call(
            attend_kernel,
            name="attend",
            grid=(clips,),
            in_specs=[smem()]
            + [one_clip(width)] * 4
            + [by_clip(1), by_clip(1), whole((width, 768)), whole((8, width))]
            + [by_clip(128), by_clip(128), whole((frames_all, 1)), whole((1, frames_all))],
            out_specs=[by_clip(768), by_clip(width)] + [one_clip(256)] * 4,
            out_shape=[
                shaped((groups, clips, slab, 768), BF),
                shaped((groups, clips, slab, width), BF),
            ]
            + [shaped((clips, slab, 256), BF)] * 4,
            compiler_params=params(),
            cost_estimate=cost(1, 2.4e9, 8e6),
        )(clip_lengths, *frame_slots, *stats, weight_qkv, vecs, cosine, sine, fcol, frow)
        return sect, act_one, [m.reshape(rows, 256) for m in mixed]

    def attend_first(frame_slots, stats, weight_qkv, vecs, outs):
        outs = jnp.stack(outs)
        outs = jnp.stack([outs, over_y(outs)], axis=1).reshape(8, piece_rows, width)
        made = attend(frame_slots, stats, weight_qkv, vecs)
        return made, outs, over_seq(outs, 2), over_y(seeds_masked)

    def middle(mixed, out_slots, vecs):
        mixed = [over_seq(mixed[m], m) if m else mixed[0] for m in range(4)]
        made = pl.pallas_call(
            middle_kernel,
            name="middle",
            in_specs=[smem()] + [vmem()] * 11,
            out_shape=[
                shaped((width, width), BF),
                shaped((rows, width), F32),
                shaped((rows, width), F32),
                shaped((rows, width), BF),
            ],
            compiler_params=params(),
            cost_estimate=cost(1, 0.6e9, 9e6),
        )(ids, *mixed, *out_slots, frames_flat, mask, vecs)
        return mixed[1:], made

    def middle_first(mixed, outs, out_x, seed_x, vecs):
        out_slots = [outs, over_seq(outs, 1), out_x, over_seq(out_x, 1)]
        return middle(mixed, out_slots, vecs), over_y(seed_x)

    def share_act(act_two, seeds):
        return gather_plane(act_two)[1:], [over_seq(seed, 1) for seed in seeds]

    def mlp(act_slots, seed_slots, mlp_pieces, vecs):
        pair_out = [None] * 4
        sums = [None] * 4
        order = (3, 1, 2, 0)
        for turn_at, pair in enumerate(order):
            acts = act_slots[2 * pair : 2 * pair + 2]
            if turn_at > 1:
                acts = after(acts, sums[order[turn_at - 2]])
            pair_out[pair] = pl.pallas_call(
                functools.partial(mlp_kernel, depth),
                name="mlp",
                out_shape=[
                    shaped((2 * rows, hidden_width), BF),
                    shaped((2 * rows, 2 * hidden_width), BF),
                    shaped((2 * rows, width), BF),
                    shaped((rows, width), BF),
                    shaped((rows, width), BF),
                ],
                scratch_shapes=[
                    pltpu.VMEM((width, 2 * hidden_width), BF),
                    pltpu.VMEM((hidden_width, width), BF),
                ],
                compiler_params=params(),
                cost_estimate=cost(2, 3.2e9, 10e6),
            )(*acts, *seed_slots[2 * pair : 2 * pair + 2], mlp_pieces, vecs)
            sums[pair] = added(pair_out[pair][3], over_seq(pair_out[pair][4], 1))
        hidden = [p[0] for p in pair_out]
        mlp_grads = pl.pallas_call(
            functools.partial(mlp_grad_kernel, depth),
            name="mlp_grad",
            out_shape=shaped((width + hidden_width, width), BF),
            scratch_shapes=[
                pltpu.VMEM((width, width), BF),
                pltpu.VMEM((hidden_width, width), BF),
            ],
            compiler_params=params(),
            cost_estimate=cost(2, 6.4e9, 17e6),
        )(*act_slots, *[p[1] for p in pair_out], *hidden, *[p[2] for p in pair_out])
        return hidden, send_plane(sums), mlp_grads

    def middle_back(back_parts, resid, attn_out, vecs, weight_out, mixed, *rest):
        grad_resid, grad_attn, *mixed_grads, middle_sums = pl.pallas_call(
            middle_back_kernel,
            name="middle_back",
            in_specs=[smem()] + [vmem()] * 10,
            out_shape=[shaped((rows, width), F32), shaped((rows, width), BF)]
            + [shaped((rows, 256), BF)] * 4
            + [shaped((8, width), F32)],
            compiler_params=params(),
            cost_estimate=cost(3, 0.6e9, 9e6),
        )(ids, *back_parts, resid, attn_out, seeds_flat, mask, vecs, weight_out)
        mixed_grads = [over_seq(g, m) if m else g for m, g in enumerate(mixed_grads)]
        out_even, out_odd, scale_sums = mlp_out(*after(rest, grad_attn))
        out_odd = over_seq(out_odd, 1)
        even, odd = pl.pallas_call(
            out_grad_kernel,
            name="out_grad",
            in_specs=[smem()] + [vmem()] * 5,
            out_shape=[shaped((2, 8, 32, width), BF)] * 2,
            scratch_shapes=[pltpu.VMEM((width, width), BF)],
            compiler_params=params(),
            cost_estimate=cost(3, 0.6e9, 4e6),
        )(ids, *after(mixed, scale_sums), grad_attn)
        odd = over_seq(odd, 1) if rings else odd
        out_sums = [added(out_even[k], out_odd[k]) for k in range(4)]
        return grad_resid, mixed_grads, even, odd, out_sums, middle_sums, scale_sums

    def attend_back(sect, mixed_grads):
        mixed_grads = [g.reshape(clips, slab, 256) for g in mixed_grads]
        grad_proj = pl.pallas_call(
            attend_back_kernel,
            name="attend_back",
            grid=(clips,),
            in_specs=[smem(), by_clip(768)]
            + [one_clip(256)] * 4
            + [by_clip(128), by_clip(128), whole((frames_all, 1)), whole((1, frames_all))],
            out_specs=by_clip(768),
            out_shape=shaped((groups, clips, slab, 768), BF),
            compiler_params=params(),
            cost_estimate=cost(3, 2.0e9, 5e6),
        )(clip_lengths, sect, *mixed_grads, cosine, sine, fcol, frow)
        grad_proj = grad_proj.reshape(groups * rows, 768)
        return grad_proj

    def qkv_grad(act_one, grad_proj, packed, *sums):
        return pl.pallas_call(
            qkv_grad_kernel,
            name="qkv_grad",
            in_specs=[smem()] + [vmem()] * 6,
            out_shape=[
                shaped((144, 1024), BF),
                shaped((2, 144, 1024), BF),
                shaped((144, 1024), BF),
                shaped((4, 144, 1024), BF),
            ],
            scratch_shapes=[pltpu.VMEM((256, 768), F32), pltpu.VMEM((16, 1024), F32)],
            compiler_params=params(),
            cost_estimate=cost(3, 1.6e9, 6e6),
        )(ids, act_one.reshape(groups * rows, width), grad_proj, packed, *sums)

    def act_grad(grad_proj, weight_qkv, frame_slots):
        return pl.pallas_call(
            act_grad_kernel,
            name="act_grad",
            out_shape=[shaped((2, rows, width), BF)] * 2 + [shaped((8, width), F32)],
            compiler_params=params(),
            cost_estimate=cost(3, 1.6e9, 7e6),
        )(grad_proj, weight_qkv, *frame_slots)

    def mlp_out(hidden, seed_slots, mlp_pieces):
        return pl.pallas_call(
            functools.partial(mlp_out_kernel, depth),
            name="mlp_out",
            out_shape=[shaped((4, rows, width), BF)] * 2 + [shaped((8, width), F32)],
            scratch_shapes=[pltpu.VMEM((hidden_width, width), BF)],
            compiler_params=params(),
            cost_estimate=cost(3, 2.2e9, 11e6),
        )(*hidden, *seed_slots, mlp_pieces)

    def last(act_near, act_far, grad_resid, vecs):
        return pl.pallas_call(
            last_kernel,
            name="last",
            out_shape=shaped((rows, width), F32),
            compiler_params=params(),
            cost_estimate=cost(3, 8e6, 4e6),
        )(act_near, act_far, frames_flat, vecs, grad_resid).reshape(frames_in.shape)

    if rings:
        packet = run(begin)
        left, right, own_y, frame_x, frame_near, mlp_first = run(to_neighbours, packet)
        far, left_y, right_y, seed_x, out_left, out_right, frame_last, stats = run(
            further, left, right, frame_x, frame_near
        )
        frame_slots = [frames_flat, frame_near, frame_x, frame_last]
        mlp_pieces = lax.all_gather(after(mlp_first, far), "z", axis=0, tiled=True)
        weight_qkv, vecs, out_far = run(
            unpack, [packet, own_y, left, left_y, right, right_y, far], out_left
        )
        outs = [w_out, out_left, out_right, out_far]
        (sect, act_one, mixed), outs, out_x, seed_y = run(
            attend_first, frame_slots, stats, weight_qkv, vecs, outs
        )
        (others, made), seed_corner = run(middle_first, mixed, outs, out_x, seed_x, vecs)
        mixed = [mixed[0], *others]
        weight_out, attn_out, resid, act_two = made
        seeds = [seeds_masked, seed_x, seed_y, seed_corner]
        others, seeds_near = run(share_act, act_two, seeds)
        act_slots = [act_two, *others]
        seed_slots = [seed for pair in zip(seeds, seeds_near) for seed in pair]
    else:
        mine = jnp.concatenate([v.reshape(1, piece_rows) for v in vectors], axis=1)
        vecs = lax.all_gather(mine, everywhere, axis=0, tiled=True).astype(F32)
        vecs = vecs.reshape(devices, 6, piece_rows).transpose(1, 0, 2).reshape(6, width)
        vecs = jnp.concatenate([vecs, jnp.zeros((2, width), F32)], axis=0)
        heads_in = w_qkv.reshape(piece_rows, 3, groups, 256).transpose(2, 0, 1, 3)
        heads_in = heads_in.reshape(groups, piece_rows, 768)
        heads_in = lax.all_to_all(heads_in, "seq", split_axis=0, concat_axis=0, tiled=True)
        heads_in = heads_in.reshape(groups * piece_rows, 768)
        weight_qkv = lax.all_gather(heads_in, ("z", "y"), axis=0, tiled=True)
        full = lax.all_gather(w_out, everywhere, axis=0, tiled=True)
        full = full.reshape(8, 4, 32, width)
        out_slots = [
            lax.dynamic_index_in_dim(full, s_here ^ m, 1, keepdims=False) for m in range(4)
        ]
        frame_slots = gather_seq(frames_flat)
        stats = norm_stats(frame_slots)
        wide_in = exchange_plane(wide_in)
        seed_slots = gather_plane(seeds_masked)
        sect, act_one, mixed = attend(frame_slots, stats, weight_qkv, vecs)
        others, made = middle(mixed, out_slots, vecs)
        mixed = [mixed[0], *others]
        weight_out, attn_out, resid, act_two = made
        act_slots = gather_plane(act_two)
        mlp_pieces = jnp.concatenate([wide_in, w_down], axis=0)
        mlp_pieces = lax.all_gather(mlp_pieces, "z", axis=0, tiled=True)
    hidden, back_parts, mlp_grads = run(mlp, act_slots, seed_slots, mlp_pieces, vecs)
    mlp_sums = lax.psum_scatter(mlp_grads, "z", scatter_dimension=0, tiled=True)
    back_parts = after(back_parts, mlp_grads)
    grad_resid, mixed_grads, even, odd, out_sums, middle_sums, scale_sums = run(
        middle_back,
        back_parts, resid, attn_out, vecs, weight_out, mixed, hidden, seed_slots, mlp_pieces,
    )
    wide_rows = 2 * groups * piece_rows
    if rings:
        halves = [added(even[k], odd[k]) for k in range(2)]
        grad_proj = attend_back(sect, after(mixed_grads, halves))
        packed = added(halves[0], over_seq(halves[1], 2))
        out_far = over_seq(jnp.stack([out_sums[1], out_sums[3]]), 2)
        act_even, act_odd, norm_sums = act_grad(grad_proj, weight_qkv, frame_slots)
        send_first, send_two, send_last, keep = qkv_grad(
            act_one, grad_proj, packed, norm_sums, middle_sums, scale_sums
        )
        act_odd = over_seq(act_odd, 1)
        act_near = added(act_even[0], act_odd[0])
        act_far = over_seq(added(act_even[1], act_odd[1]), 2)
        first = added(keep[0], over_y(send_first))
        two = over_y(after(send_two, first))
        out_near = out_sums[0].astype(F32) + out_far[0].astype(F32)
        out_side = added(out_sums[2], out_far[1])
        passed = over_z(after(first, mlp_sums, out_side), 1)
        blocks = [added(added(keep[1], two[0]), passed), added(keep[2], two[1])]
        send_last = over_y(after(send_last, two))
        out_side = over_y(after(out_side, two))
        left, right = over_z(blocks[0], 1), over_z(blocks[1], -1)
        input_grad = last(act_near, act_far, grad_resid, vecs)
        wide_out = exchange_plane(mlp_sums[:wide_rows].reshape(2 * groups, piece_rows, 1024))
        total = added(keep[3], send_last).astype(F32) + left.astype(F32) + right.astype(F32)
        total = after(total, input_grad, wide_out)
        parts = pl.pallas_call(
            prepare_kernel,
            name="prepare",
            out_shape=shaped((4, 48, 768), BF),
            compiler_params=params(),
            cost_estimate=cost(3, 1e6, 1e6),
        )(total)
        parts = lax.all_to_all(parts, "seq", split_axis=0, concat_axis=0, tiled=True)
        sum_qkv, sums = pl.pallas_call(
            finish_kernel,
            name="finish",
            out_shape=[shaped(w_qkv.shape, F32), shaped((8, 128), F32)],
            compiler_params=params(),
            cost_estimate=cost(3, 1e6, 1e6),
        )(parts)
        sums = sums[:, :piece_rows]
        sum_out = jnp.concatenate(
            [total[piece_rows * q : piece_rows * (q + 1), 768:] for q in range(4)], axis=1
        )
        mlp_result = out_near + out_side.astype(F32)
    else:
        packed = even[0]
        grad_proj = attend_back(sect, mixed_grads)
        act_even, act_odd, norm_sums = act_grad(grad_proj, weight_qkv, frame_slots)
        send_first, send_two, send_last, keep = qkv_grad(
            act_one, grad_proj, packed, norm_sums, middle_sums, scale_sums
        )
        act_odd = over_seq(act_odd, 1)
        act_near = added(act_even[0], act_odd[0])
        act_far = over_seq(added(act_even[1], act_odd[1]), 2)
        input_grad = last(act_near, act_far, grad_resid, vecs)
        sums = jnp.concatenate([norm_sums[0:2], middle_sums[0:3], scale_sums[0:1]], axis=0)
        sums = lax.psum(sums, everywhere)
        sums = lax.dynamic_index_in_dim(
            sums.reshape(6, devices, piece_rows), device, 1, keepdims=False
        )
        sends = jnp.concatenate([send_first[None], send_two, send_last[None]])
        full = jnp.stack([keep, sends], axis=1)[:, :, :128, :768].reshape(width, 768)
        sum_qkv = lax.psum_scatter(full, ("z", "y"), scatter_dimension=0, tiled=True)
        sum_qkv = sum_qkv.reshape(groups, piece_rows, 768)
        sum_qkv = lax.all_to_all(sum_qkv, "seq", split_axis=0, concat_axis=0, tiled=True)
        sum_qkv = sum_qkv.reshape(groups, piece_rows, 3, 256).transpose(1, 2, 0, 3)
        sum_qkv = sum_qkv.reshape(w_qkv.shape).astype(F32)
        full = jnp.stack([even[0], odd[0], even[1], odd[1]])
        full = jnp.stack(
            [lax.dynamic_index_in_dim(full, s_here ^ m, 0, keepdims=False) for m in range(4)], axis=1
        ).reshape(width, width)
        sum_out = lax.psum_scatter(full, everywhere, scatter_dimension=0, tiled=True).astype(F32)
        wide_out = exchange_plane(mlp_sums[:wide_rows].reshape(2 * groups, piece_rows, 1024))
        mlp_result = sum(part.astype(F32) for part in send_plane(out_sums))

    layer_out = (resid + mask * vecs[5:6, :] * mlp_result).astype(BF).reshape(frames_in.shape)
    wide_out = wide_out.reshape(2 * groups, piece_rows, 2, depth, units).transpose(1, 2, 3, 0, 4)
    sum_gate_up = wide_out.reshape(w_gate_up.shape).astype(F32)
    sum_down = mlp_sums[wide_rows:].astype(F32)

    return (
        layer_out,
        input_grad,
        sums[0],
        sums[1],
        sum_qkv,
        sum_out,
        sums[4],
        sums[2],
        sums[3],
        sum_gate_up,
        sum_down,
        sums[5],
    )


def solution(mesh):
    clip_groups, groups = mesh.shape["clips"], mesh.shape["seq"]
    depth = clip_groups // 2
    split = Mesh(mesh.devices.reshape(depth, 2, groups), ("z", "y", "seq"))
    clips, everywhere = ("z", "y"), ("z", "y", "seq")
    by_frame, by_clip = P(clips, "seq", None), P(clips)
    by_row, by_entry = P(everywhere, None), P(everywhere)
    return jax.shard_map(
        functools.partial(on_device, rings=depth == 4 and groups == 4),
        mesh=split,
        in_specs=(
            by_frame, by_frame, by_clip, by_clip, by_entry, by_entry, by_row, by_row,
            by_entry, by_entry, by_entry, by_row, by_row, by_entry,
        ),
        out_specs=(
            by_frame, by_frame, by_entry, by_entry, by_row, by_row, by_entry, by_entry,
            by_entry, by_row, by_row, by_entry,
        ),
        check_vma=False,
    )
```

```python
import functools

import jax
import jax.numpy as jnp
import numpy as np
from jax import lax
from jax.experimental import pallas as pl
from jax.experimental.pallas import tpu as pltpu
from jax.sharding import Mesh
from jax.sharding import PartitionSpec as P

H = 16
HD = 64
FF = 4096
WIN = 128
NEG_FILL = -1000000000.0
EPS = 1e-05
BF = jnp.bfloat16
F32 = jnp.float32
VMEM_BYTES = 56 * 1024 * 1024
COST_SCALE = (10, 10, 10, 10, 0.01)

ID_SEQ, ID_Y, ID_POS, ID_DEST, ID_CPOS = 0, 1, 2, 10, 14


def dot_nn(left, right):
    return jnp.dot(left, right, preferred_element_type=F32)


def dot_nt(left, right):
    return lax.dot_general(left, right, (((1,), (1,)), ((), ())), preferred_element_type=F32)


def dot_tn(left, right):
    return lax.dot_general(left, right, (((0,), (0,)), ((), ())), preferred_element_type=F32)


def smem():
    return pl.BlockSpec(memory_space=pltpu.SMEM)


def vmem():
    return pl.BlockSpec(memory_space=pltpu.VMEM)


def shaped(shape, dtype):
    return jax.ShapeDtypeStruct(shape, dtype)


def params():
    return pltpu.CompilerParams(vmem_limit_bytes=VMEM_BYTES)


def cost(phase, flops, moved):
    scale = COST_SCALE[phase]
    return pl.CostEstimate(
        flops=int(flops * scale), bytes_accessed=int(moved * scale), transcendentals=0
    )


def rows_at(index, size):
    return pl.ds(pl.multiple_of(index * size, size), size)


def normed(values):
    center = values - jnp.mean(values, axis=-1, keepdims=True)
    spread = lax.rsqrt(jnp.mean(center * center, axis=-1, keepdims=True) + EPS)
    return center * spread, spread


def pack_kernel(ids, weight, vector, *outs):
    me = ids[ID_SEQ]
    for slot, out in enumerate(outs):
        other = jnp.bitwise_xor(me, slot)
        for part in range(3):
            start = pl.multiple_of(part * 1024 + other * 256, 256)
            out[0:32, 256 * part : 256 * part + 256] = weight[:, pl.ds(start, 256)]
        out[32:48, 0:128] = vector[...]
        out[32:48, 128:768] = jnp.zeros((16, 640), BF)


def packet_kernel(s0, s1, s2, s3, packet):
    total = jnp.zeros((16, 128), F32)
    for slot, ref in enumerate((s0, s1, s2, s3)):
        packet[32 * slot : 32 * slot + 32, :] = ref[0:32, :]
        total = total + ref[32:48, 0:128].astype(F32)
    packet[128:144, 0:128] = total.astype(BF)
    packet[128:144, 128:768] = jnp.zeros((16, 640), BF)


def unpack_kernel(ids, *refs):
    pieces, (weight, vecs) = refs[:8], refs[8:]
    me = ids[ID_SEQ]
    for place, piece in enumerate(pieces):
        spot = ids[ID_POS + place]
        for slot in range(4):
            start = pl.multiple_of(spot * 128 + jnp.bitwise_xor(me, slot) * 32, 32)
            weight[pl.ds(start, 32), :] = piece[32 * slot : 32 * slot + 32, :]
        lanes = pl.ds(pl.multiple_of(spot * 128, 128), 128)
        vecs[:, lanes] = piece[128:144, 0:128].astype(F32)[0:8, :]


def norm_stats_kernel(x0, x1, x2, x3, mean, spread):
    for slot, frames in enumerate((x0, x1, x2, x3)):
        values = frames[...].astype(F32)
        middle = jnp.mean(values, axis=-1, keepdims=True)
        center = values - middle
        mean[slot] = middle
        spread[slot] = lax.rsqrt(jnp.mean(center * center, axis=-1, keepdims=True) + EPS)


def visible_bias(fcol, frow, length):
    gap = jnp.abs(fcol[...] - frow[...])
    seen = (gap <= WIN // 2) & (frow[...] < length.astype(F32))
    return jnp.where(seen, 0.0, NEG_FILL)


def turn(values, cosine, sine, lower):
    swapped = jnp.where(lower, pltpu.roll(values, 96, 1), pltpu.roll(values, 32, 1))
    return values * cosine + swapped * sine


def lane_masks():
    lane = lax.broadcasted_iota(jnp.int32, (1, 128), 1)
    lower = lane % 64 < 32
    return lower, [(lane // 64 == half).astype(F32) for half in (0, 1)]


def attend_kernel(
    lens, x0, x1, x2, x3, mean, spread, weight, vecs, cosine, sine, fcol, frow,
    sect, act, m0, m1, m2, m3,
):
    clip = pl.program_id(0)
    slab, width = x0.shape[1:]
    rows = 4 * slab
    frames = jnp.concatenate([x[0] for x in (x0, x1, x2, x3)], axis=0).astype(F32)
    frames = (frames - mean[...].reshape(rows, 1)) * spread[...].reshape(rows, 1)
    normal = (frames * vecs[0:1, :] + vecs[1:2, :]).astype(BF)
    act[...] = normal.reshape(act.shape)
    projected = dot_nn(normal, weight[...])
    cos_rows = cosine[...].reshape(rows, 128)
    sin_rows = sine[...].reshape(rows, 128)
    lower, masks = lane_masks()
    lower = jnp.broadcast_to(lower, (rows, 128))
    chunks = []
    for place in range(6):
        chunk = projected[:, 128 * place : 128 * place + 128]
        if place < 4:
            chunk = turn(chunk, cos_rows, sin_rows, lower)
        chunk = chunk.astype(BF)
        chunks.append(chunk)
        sect[:, 0, :, 128 * place : 128 * place + 128] = chunk.reshape(-1, slab, 128)
    bias = visible_bias(fcol, frow, lens[clip])
    for pair in range(2):
        total = jnp.zeros((rows, 128), F32)
        for half in range(2):
            mask = masks[half].astype(BF)
            scores = dot_nt(chunks[pair] * mask, chunks[2 + pair]) * HD ** (-0.5) + bias
            expo = jnp.exp(scores - jnp.max(scores, axis=-1, keepdims=True))
            weights = (expo * (1.0 / jnp.sum(expo, axis=-1, keepdims=True))).astype(BF)
            total = total + dot_nn(weights, chunks[4 + pair] * mask)
        total = total.astype(BF)
        for slot, out in enumerate((m0, m1, m2, m3)):
            out[0, :, 128 * pair : 128 * pair + 128] = total[slab * slot : slab * (slot + 1)]


def attend_back_kernel(lens, sect, g0, g1, g2, g3, cosine, sine, fcol, frow, grad):
    clip = pl.program_id(0)
    slab = sect.shape[2]
    rows = sect.shape[0] * slab
    cos_rows = cosine[...].reshape(rows, 128)
    sin_rows = -sine[...].reshape(rows, 128)
    lower, masks = lane_masks()
    lower = jnp.broadcast_to(lower, (rows, 128))
    bias = visible_bias(fcol, frow, lens[clip])

    def part(place):
        return sect[:, 0, :, 128 * place : 128 * place + 128].reshape(rows, 128)

    def put(place, values):
        grad[:, 0, :, 128 * place : 128 * place + 128] = values.astype(BF).reshape(-1, slab, 128)

    for pair in range(2):
        queries, keys_in, values_in = part(pair), part(2 + pair), part(4 + pair)
        mixed_grad = jnp.concatenate(
            [g[0, :, 128 * pair : 128 * pair + 128] for g in (g0, g1, g2, g3)], axis=0
        )
        grad_q = jnp.zeros((rows, 128), F32)
        grad_k = jnp.zeros((rows, 128), F32)
        grad_v = jnp.zeros((rows, 128), F32)
        for half in range(2):
            mask = masks[half].astype(BF)
            query = queries * mask
            upper = mixed_grad * mask
            scores = dot_nt(query, keys_in) * HD ** (-0.5) + bias
            expo = jnp.exp(scores - jnp.max(scores, axis=-1, keepdims=True))
            probs = expo * (1.0 / jnp.sum(expo, axis=-1, keepdims=True))
            grad_v = grad_v + dot_tn(probs.astype(BF), upper)
            grad_probs = dot_nt(upper, values_in)
            centre = jnp.sum(probs * grad_probs, axis=-1, keepdims=True)
            grad_scores = (probs * (grad_probs - centre)).astype(BF)
            grad_q = grad_q + dot_nn(grad_scores, keys_in * mask)
            grad_k = grad_k + dot_tn(grad_scores, query)
        grad_q = (grad_q * HD ** (-0.5)).astype(BF).astype(F32)
        grad_k = (grad_k * HD ** (-0.5)).astype(BF).astype(F32)
        put(pair, turn(grad_q, cos_rows, sin_rows, lower))
        put(2 + pair, turn(grad_k, cos_rows, sin_rows, lower))
        put(4 + pair, grad_v)


def middle_kernel(
    ids, m0, m1, m2, m3, w0, w1, w2, w3, frames, mask, vecs, weight, attn_out, resid, act
):
    me = ids[ID_SEQ]
    for slot, packed in enumerate((w0, w1, w2, w3)):
        other = jnp.bitwise_xor(me, slot)
        for place in range(8):
            start = pl.multiple_of(ids[ID_POS + place] * 128 + other * 32, 32)
            weight[pl.ds(start, 32), :] = packed[place]
    total = jnp.zeros(attn_out.shape, F32)
    for slot, mixed in enumerate((m0, m1, m2, m3)):
        block = weight[rows_at(jnp.bitwise_xor(me, slot), 256), :]
        total = total + dot_nn(mixed[...], block)
    attn_out[...] = total
    summed = frames[...].astype(F32) + mask[...] * vecs[2:3, :] * total
    resid[...] = summed
    xhat, _ = normed(summed)
    act[...] = (xhat * vecs[3:4, :] + vecs[4:5, :]).astype(BF)


def middle_back_kernel(
    ids, q0, q1, q2, q3, resid, attn_out, grad_in, mask, vecs, weight,
    grad_resid, grad_attn, g0, g1, g2, g3, sums,
):
    me = ids[ID_SEQ]
    grad_act = q0[...].astype(F32) + q1[...].astype(F32) + q2[...].astype(F32) + q3[...].astype(F32)
    xhat, spread = normed(resid[...])
    sums[0:1, :] = jnp.sum(grad_act * xhat, axis=0, keepdims=True)
    sums[1:2, :] = jnp.sum(grad_act, axis=0, keepdims=True)
    pulled = grad_act * vecs[3:4, :]
    pulled = spread * (
        pulled
        - jnp.mean(pulled, axis=-1, keepdims=True)
        - xhat * jnp.mean(pulled * xhat, axis=-1, keepdims=True)
    )
    total = grad_in[...].astype(F32) + pulled
    grad_resid[...] = total
    masked = mask[...] * total
    sums[2:3, :] = jnp.sum(masked * attn_out[...], axis=0, keepdims=True)
    sums[3:8, :] = jnp.zeros((5, sums.shape[1]), F32)
    scaled = (masked * vecs[2:3, :]).astype(BF)
    grad_attn[...] = scaled
    for slot, out in enumerate((g0, g1, g2, g3)):
        block = weight[rows_at(jnp.bitwise_xor(me, slot), 256), :]
        out[...] = dot_nt(scaled, block).astype(BF)


def out_grad_kernel(ids, m0, m1, m2, m3, grad_attn, even, odd, held):
    me = ids[ID_SEQ]
    for slot, mixed in enumerate((m0, m1, m2, m3)):
        held[rows_at(jnp.bitwise_xor(me, slot), 256), :] = dot_tn(mixed[...], grad_attn[...]).astype(
            BF
        )
    for slot in range(4):
        other = jnp.bitwise_xor(me, slot)
        out = odd if slot % 2 else even
        for place in range(8):
            start = pl.multiple_of(ids[ID_CPOS + place] * 128 + other * 32, 32)
            out[slot // 2, place] = held[pl.ds(start, 32), :]


def piece_parts(depth, held, place):
    wide, down = 1024 // depth, held // depth
    start = (wide + down) * place
    return (
        (slice(start, start + wide), slice(wide * place, wide * place + wide)),
        (slice(start + wide, start + wide + down), slice(down * place, down * place + down)),
    )


def spread_pieces(depth, pieces, w_in, w_down):
    for place in range(depth):
        upper, lower = piece_parts(depth, w_down.shape[0], place)
        if w_in is not None:
            w_in[upper[1], :] = pieces[upper[0], :]
        w_down[lower[1], :] = pieces[lower[0], :]


def mlp_kernel(
    depth, a0, a1, o0, o1, pieces, vecs, hidden, grads, grad_mlp, even, odd, w_in, w_down
):
    spread_pieces(depth, pieces, w_in, w_down)
    width = hidden.shape[1]
    for slot, (act, seed, out) in enumerate(((a0, o0, even), (a1, o1, odd))):
        here = slice(256 * slot, 256 * slot + 256)
        gate_up = dot_nn(act[...], w_in[...])
        gate, up = gate_up[:, :width], gate_up[:, width:]
        pulled = (vecs[5:6, :] * seed[...].astype(F32)).astype(BF)
        grad_mlp[here, :] = pulled
        grad_hidden = dot_nt(pulled, w_down[...])
        sig = jax.nn.sigmoid(gate)
        silu = gate * sig
        hidden[here, :] = (silu * up).astype(BF)
        grad_gate = grad_hidden * up * sig * (1.0 + gate * (1.0 - sig))
        grads[here, :width] = grad_gate.astype(BF)
        grads[here, width:] = (grad_hidden * silu).astype(BF)
        out[...] = dot_nt(grads[here, :], w_in[...]).astype(BF)


def mlp_grad_kernel(depth, *refs):
    acts, refs = refs[:8], refs[8:]
    grads, refs = refs[:4], refs[4:]
    hidden, refs = refs[:4], refs[4:]
    grad_mlp, (out, upper, lower) = refs[:4], refs[4:]
    for block in range(4):
        wide = slice(256 * block, 256 * block + 256)
        narrow = slice(128 * block, 128 * block + 128)
        total = jnp.zeros((256, out.shape[1]), F32)
        rest = jnp.zeros((128, out.shape[1]), F32)
        for pair in range(4):
            for slot in range(2):
                here = slice(256 * slot, 256 * slot + 256)
                total = total + dot_tn(acts[2 * pair + slot][:, wide], grads[pair][here, :])
            rest = rest + dot_tn(hidden[pair][:, narrow], grad_mlp[pair][...])
        upper[wide, :] = total.astype(BF)
        lower[narrow, :] = rest.astype(BF)
    for place in range(depth):
        first, second = piece_parts(depth, lower.shape[0], place)
        out[first[0], :] = upper[first[1], :]
        out[second[0], :] = lower[second[1], :]


def mlp_out_kernel(depth, *refs):
    hidden, refs = refs[:4], refs[4:]
    seeds, refs = refs[:8], refs[8:]
    pieces, refs = refs[0], refs[1:]
    even, odd, sums, w_down = refs
    spread_pieces(depth, pieces, None, w_down)
    total = jnp.zeros((1, sums.shape[1]), F32)
    for slot in range(8):
        here = slice(256 * (slot % 2), 256 * (slot % 2) + 256)
        result = dot_nn(hidden[slot // 2][here, :], w_down[...])
        out = odd if slot % 2 else even
        out[slot // 2] = result.astype(BF)
        total = total + jnp.sum(result * seeds[slot][...].astype(F32), axis=0, keepdims=True)
    sums[...] = jnp.concatenate([total, jnp.zeros((7, sums.shape[1]), F32)], axis=0)


def qkv_grad_kernel(
    ids, act, grad, packed, norm_sums, middle_sums, scale_sums, send_first, send_two, send_last, keep, held, sums
):
    sums[0:8, :] = jnp.concatenate(
        [norm_sums[0:2, :], middle_sums[0:3, :], scale_sums[0:1, :], jnp.zeros((2, 1024), F32)],
        axis=0,
    )
    sums[8:16, :] = jnp.zeros((8, 1024), F32)
    y_here = ids[ID_Y]
    for place in range(4):
        block = ids[ID_DEST + place]
        wide = pl.ds(pl.multiple_of(block * 256, 256), 256)
        held[...] = dot_tn(act[:, wide], grad[...])
        send = (send_first, send_two.at[0], send_two.at[1], send_last)[place]
        for half, out in ((0, keep.at[place]), (1, send)):
            row = y_here if half == 0 else 1 - y_here
            out[0:128, 0:768] = held[rows_at(row, 128), :].astype(BF)
            for quarter in range(4):
                out[32 * quarter : 32 * quarter + 32, 768:1024] = packed[
                    2 * place + half, :, 256 * quarter : 256 * quarter + 256
                ]
            lanes = pl.ds(pl.multiple_of(block * 256 + row * 128, 128), 128)
            out[128:144, 0:128] = sums[:, lanes].astype(BF)
            out[128:144, 128:1024] = jnp.zeros((16, 896), BF)


def prepare_kernel(total, parts):
    for place in range(4):
        parts[place, 0:32, :] = total[32 * place : 32 * place + 32, 0:768].astype(BF)
        block = total[128:144, 0:128]
        block = pltpu.roll(block, 128 - 32 * place, 1) if place else block
        parts[place, 32:48, 0:128] = block.astype(BF)
        parts[place, 32:48, 128:768] = jnp.zeros((16, 640), BF)


def finish_kernel(parts, out, sums):
    total = jnp.zeros((16, 128), F32)
    for place in range(4):
        for part in range(3):
            start = 1024 * part + 256 * place
            here = 256 * part
            out[:, start : start + 256] = parts[place, 0:32, here : here + 256].astype(F32)
        total = total + parts[place, 32:48, 0:128].astype(F32)
    sums[...] = total[0:8, :]


def act_grad_kernel(grad, weight, x0, x1, x2, x3, even, odd, sums):
    gain_sum = jnp.zeros((1, sums.shape[1]), F32)
    bias_sum = jnp.zeros((1, sums.shape[1]), F32)
    for slot, frames in enumerate((x0, x1, x2, x3)):
        result = dot_nt(grad[256 * slot : 256 * slot + 256, :], weight[...])
        out = odd if slot % 2 else even
        out[slot // 2] = result.astype(BF)
        xhat, _ = normed(frames[...].astype(F32))
        gain_sum = gain_sum + jnp.sum(result * xhat, axis=0, keepdims=True)
        bias_sum = bias_sum + jnp.sum(result, axis=0, keepdims=True)
    sums[...] = jnp.concatenate(
        [gain_sum, bias_sum, jnp.zeros((6, sums.shape[1]), F32)], axis=0
    )


def last_kernel(u, v, frames, vecs, grad_resid, out):
    grad_act = u[...].astype(F32) + v[...].astype(F32)
    xhat, spread = normed(frames[...].astype(F32))
    pulled = grad_act * vecs[0:1, :]
    out[...] = grad_resid[...] + spread * (
        pulled
        - jnp.mean(pulled, axis=-1, keepdims=True)
        - xhat * jnp.mean(pulled * xhat, axis=-1, keepdims=True)
    )


def added(left, right):
    return (left.astype(F32) + right.astype(F32)).astype(BF)


def after(value, *first):
    return lax.optimization_barrier((value, first))[0]


def on_device(
    frames_in,
    output_grad,
    clip_kinds,
    clip_lengths,
    norm1_gain,
    norm1_bias,
    w_qkv,
    w_out,
    attn_scale,
    norm2_gain,
    norm2_bias,
    w_gate_up,
    w_down,
    mlp_scale,
    *,
    rings,
):
    depth = lax.axis_size("z")
    groups = lax.axis_size("seq")
    z_here, y_here, s_here = lax.axis_index("z"), lax.axis_index("y"), lax.axis_index("seq")
    everywhere = ("z", "y", "seq")
    plane = ("y", "seq")
    clips, slab, width = frames_in.shape
    rows = clips * slab
    device = (z_here * 2 + y_here) * groups + s_here
    devices = depth * 2 * groups
    piece_rows = w_qkv.shape[0]

    def over_seq(array_in, flip):
        return lax.ppermute(array_in, "seq", [(i, i ^ flip) for i in range(groups)])

    def over_y(array_in):
        return lax.ppermute(array_in, "y", [(0, 1), (1, 0)])

    def over_corner(array_in):
        pairs = [
            (y * groups + s, (1 - y) * groups + (s ^ 2)) for y in range(2) for s in range(groups)
        ]
        return lax.ppermute(array_in, plane, pairs)

    def over_z(array_in, step):
        return lax.ppermute(array_in, "z", [(i, (i + step) % depth) for i in range(depth)])

    def gather_z(array_in):
        left, right = over_z(array_in, 1), over_z(array_in, -1)
        return [array_in, left, right, over_z(left, 1)]

    def scatter_z(blocks):
        passed = added(blocks[1], over_z(blocks[0], 1))
        left, right = over_z(passed, 1), over_z(blocks[2], -1)
        return blocks[3].astype(F32) + left.astype(F32) + right.astype(F32)

    def gather_seq(array_in):
        near, far = over_seq(array_in, 1), over_seq(array_in, 2)
        return [array_in, near, far, over_seq(far, 1)]

    def gather_plane(array_in):
        slots = [array_in, over_seq(array_in, 1)]
        beside, across = over_seq(array_in, 2), over_y(array_in)
        for arrived in (beside, across, over_corner(array_in)):
            slots += [arrived, over_seq(arrived, 1)]
        return slots

    def scatter_plane(slots):
        return send_plane(
            [added(slots[2 * p], over_seq(slots[2 * p + 1], 1)) for p in range(4)]
        )

    def send_plane(sums):
        return [sums[0], over_seq(sums[1], 2), over_y(sums[2]), over_corner(sums[3])]

    def exchange_plane(array_in):
        parts = lax.all_to_all(array_in, plane, split_axis=0, concat_axis=0, tiled=True)
        return parts.reshape(-1, array_in.shape[-1])

    def norm_stats(slots):
        return pl.pallas_call(
            norm_stats_kernel,
            name="norm_stats",
            out_shape=[shaped((groups, rows, 1), F32)] * 2,
            compiler_params=params(),
            cost_estimate=cost(0, 16e6, 6e6),
        )(*slots)

    if rings:
        came = [(z_here + k) % depth for k in (0, -1, 1, -2)]
        dest = [(z_here + k) % depth for k in (2, 1, -1, 0)]
        pos = [came[k] * 2 + (y_here if h == 0 else 1 - y_here) for k in range(4) for h in (0, 1)]
        y_row = y_here
    else:
        dest = [jnp.int32(k) for k in range(4)]
        pos = [jnp.int32(k) for k in range(8)]
        y_row = jnp.int32(0)
    cpos = [dest[k] * 2 + (y_row if h == 0 else 1 - y_row) for k in range(4) for h in (0, 1)]
    ids = jnp.stack([s_here, y_row, *pos, *dest, *cpos]).astype(jnp.int32)

    frame_times = s_here * slab + jnp.arange(slab)
    mask = (frame_times[None, :] < clip_lengths[:, None]).astype(F32).reshape(rows, 1)
    slot_times = (
        (jnp.arange(groups) ^ s_here)[:, None] * slab + jnp.arange(slab)[None, :]
    ).astype(F32)
    rates = 1.0 + clip_kinds.astype(F32)
    positions = slot_times[:, None, :] * rates[None, :, None]
    lane = jnp.arange(128)
    inv_freq = 10000.0 ** (-2.0 * (lane % 32).astype(F32) / HD)
    angles = positions[..., None] * inv_freq
    cosine = jnp.cos(angles)
    sine = jnp.sin(angles) * jnp.where(lane % 64 < 32, -1.0, 1.0)
    fcol = slot_times.reshape(groups * slab, 1)
    frow = slot_times.reshape(1, groups * slab)

    frames_flat = frames_in.reshape(rows, width)
    seeds_flat = output_grad.reshape(rows, width)
    seeds_masked = (seeds_flat.astype(F32) * mask).astype(BF)
    vectors = (norm1_gain, norm1_bias, attn_scale, norm2_gain, norm2_bias, mlp_scale)
    units = w_down.shape[0]
    hidden_width = FF // (2 * groups)
    frames_all = groups * slab
    wide_in = w_gate_up.reshape(piece_rows, 2, depth, 2 * groups, units).transpose(3, 0, 1, 2, 4)
    wide_in = wide_in.reshape(2 * groups, piece_rows, 1024)

    def by_clip(last):
        return pl.BlockSpec((groups, 1, slab, last), lambda c: (0, c, 0, 0))

    def one_clip(last):
        return pl.BlockSpec((1, slab, last), lambda c: (c, 0, 0))

    def whole(shape):
        return pl.BlockSpec(shape, lambda c: (0,) * len(shape))

    def begin():
        mine = jnp.pad(jnp.stack(vectors), ((0, 10), (0, 96)))
        mine = jnp.roll(mine, s_here * 32, axis=1)
        slots = pl.pallas_call(
            pack_kernel,
            name="pack",
            in_specs=[smem(), vmem(), vmem()],
            out_shape=[shaped((48, 768), BF)] * 4,
            compiler_params=params(),
            cost_estimate=cost(0, 1e6, 5e5),
        )(ids, w_qkv, mine)
        slots = [slots[0]] + [over_seq(slots[m], m) for m in (2, 3, 1)]
        packet = pl.pallas_call(
            packet_kernel,
            name="packet",
            out_shape=shaped((144, 768), BF),
            compiler_params=params(),
            cost_estimate=cost(0, 1e6, 8e5),
        )(*after((slots[0], slots[3], slots[1], slots[2]), cosine, sine, fcol, frow))
        return packet

    def to_neighbours(packet):
        wide = exchange_plane(wide_in)
        return (
            over_z(packet, 1),
            over_z(packet, -1),
            over_y(packet),
            over_seq(frames_flat, 2),
            over_seq(frames_flat, 1),
            jnp.concatenate([wide, w_down], axis=0),
        )

    def further(left, right, frame_x, frame_near):
        frame_last = over_seq(frame_x, 1)
        return (
            over_z(left, 1),
            over_y(left),
            over_y(right),
            over_seq(seeds_masked, 2),
            over_z(w_out, 1),
            over_z(w_out, -1),
            frame_last,
            norm_stats([frames_flat, frame_near, frame_x, frame_last]),
        )

    def unpack(pieces, out):
        last_y = over_y(pieces[-1])
        out_last = over_z(out, 1)
        weight_qkv, vecs = pl.pallas_call(
            unpack_kernel,
            name="unpack",
            in_specs=[smem()] + [vmem()] * 8,
            out_shape=[shaped((width, 768), BF), shaped((8, width), F32)],
            compiler_params=params(),
            cost_estimate=cost(1, 1e6, 4e6),
        )(ids, *pieces, last_y)
        return weight_qkv, vecs, out_last

    def attend(frame_slots, stats, weight_qkv, vecs):
        frame_slots = [slot.reshape(clips, slab, width) for slot in frame_slots]
        stats = [stat.reshape(groups, clips, slab, 1) for stat in stats]
        sect, act_one, *mixed = pl.pallas_call(
            attend_kernel,
            name="attend",
            grid=(clips,),
            in_specs=[smem()]
            + [one_clip(width)] * 4
            + [by_clip(1), by_clip(1), whole((width, 768)), whole((8, width))]
            + [by_clip(128), by_clip(128), whole((frames_all, 1)), whole((1, frames_all))],
            out_specs=[by_clip(768), by_clip(width)] + [one_clip(256)] * 4,
            out_shape=[
                shaped((groups, clips, slab, 768), BF),
                shaped((groups, clips, slab, width), BF),
            ]
            + [shaped((clips, slab, 256), BF)] * 4,
            compiler_params=params(),
            cost_estimate=cost(1, 2.4e9, 8e6),
        )(clip_lengths, *frame_slots, *stats, weight_qkv, vecs, cosine, sine, fcol, frow)
        return sect, act_one, [m.reshape(rows, 256) for m in mixed]

    def attend_first(frame_slots, stats, weight_qkv, vecs, outs):
        outs = jnp.stack(outs)
        outs = jnp.stack([outs, over_y(outs)], axis=1).reshape(8, piece_rows, width)
        made = attend(frame_slots, stats, weight_qkv, vecs)
        return made, outs, over_seq(outs, 2), over_y(seeds_masked)

    def middle(mixed, out_slots, vecs):
        mixed = [over_seq(mixed[m], m) if m else mixed[0] for m in range(4)]
        made = pl.pallas_call(
            middle_kernel,
            name="middle",
            in_specs=[smem()] + [vmem()] * 11,
            out_shape=[
                shaped((width, width), BF),
                shaped((rows, width), F32),
                shaped((rows, width), F32),
                shaped((rows, width), BF),
            ],
            compiler_params=params(),
            cost_estimate=cost(1, 0.6e9, 9e6),
        )(ids, *mixed, *out_slots, frames_flat, mask, vecs)
        return mixed[1:], made

    def middle_first(mixed, outs, out_x, seed_x, vecs):
        out_slots = [outs, over_seq(outs, 1), out_x, over_seq(out_x, 1)]
        return middle(mixed, out_slots, vecs), over_y(seed_x)

    def share_act(act_two, seeds):
        return gather_plane(act_two)[1:], [over_seq(seed, 1) for seed in seeds]

    def mlp(act_slots, seed_slots, mlp_pieces, vecs):
        pair_out = [None] * 4
        sums = [None] * 4
        order = (3, 1, 2, 0)
        for turn_at, pair in enumerate(order):
            acts = act_slots[2 * pair : 2 * pair + 2]
            if turn_at > 1:
                acts = after(acts, sums[order[turn_at - 2]])
            pair_out[pair] = pl.pallas_call(
                functools.partial(mlp_kernel, depth),
                name="mlp",
                out_shape=[
                    shaped((2 * rows, hidden_width), BF),
                    shaped((2 * rows, 2 * hidden_width), BF),
                    shaped((2 * rows, width), BF),
                    shaped((rows, width), BF),
                    shaped((rows, width), BF),
                ],
                scratch_shapes=[
                    pltpu.VMEM((width, 2 * hidden_width), BF),
                    pltpu.VMEM((hidden_width, width), BF),
                ],
                compiler_params=params(),
                cost_estimate=cost(2, 3.2e9, 10e6),
            )(*acts, *seed_slots[2 * pair : 2 * pair + 2], mlp_pieces, vecs)
            sums[pair] = added(pair_out[pair][3], over_seq(pair_out[pair][4], 1))
        hidden = [p[0] for p in pair_out]
        back_parts = send_plane(sums)
        mlp_grads = pl.pallas_call(
            functools.partial(mlp_grad_kernel, depth),
            name="mlp_grad",
            out_shape=shaped((width + hidden_width, width), BF),
            scratch_shapes=[
                pltpu.VMEM((width, width), BF),
                pltpu.VMEM((hidden_width, width), BF),
            ],
            compiler_params=params(),
            cost_estimate=cost(2, 6.4e9, 17e6),
        )(*act_slots, *[p[1] for p in pair_out], *hidden, *[p[2] for p in pair_out])
        return hidden, back_parts, mlp_grads

    def middle_back(back_parts, resid, attn_out, vecs, weight_out, mixed, *rest):
        grad_resid, grad_attn, *mixed_grads, middle_sums = pl.pallas_call(
            middle_back_kernel,
            name="middle_back",
            in_specs=[smem()] + [vmem()] * 10,
            out_shape=[shaped((rows, width), F32), shaped((rows, width), BF)]
            + [shaped((rows, 256), BF)] * 4
            + [shaped((8, width), F32)],
            compiler_params=params(),
            cost_estimate=cost(3, 0.6e9, 9e6),
        )(ids, *back_parts, resid, attn_out, seeds_flat, mask, vecs, weight_out)
        mixed_grads = [over_seq(g, m) if m else g for m, g in enumerate(mixed_grads)]
        out_even, out_odd, scale_sums = mlp_out(*after(rest, grad_attn))
        out_odd = over_seq(out_odd, 1)
        even, odd = pl.pallas_call(
            out_grad_kernel,
            name="out_grad",
            in_specs=[smem()] + [vmem()] * 5,
            out_shape=[shaped((2, 8, 32, width), BF)] * 2,
            scratch_shapes=[pltpu.VMEM((width, width), BF)],
            compiler_params=params(),
            cost_estimate=cost(4, 0.6e9, 4e6),
        )(ids, *after(mixed, scale_sums), grad_attn)
        odd = over_seq(odd, 1) if rings else odd
        out_sums = [added(out_even[k], out_odd[k]) for k in range(4)]
        return grad_resid, mixed_grads, even, odd, out_sums, middle_sums, scale_sums

    def attend_back(sect, mixed_grads):
        mixed_grads = [g.reshape(clips, slab, 256) for g in mixed_grads]
        grad_proj = pl.pallas_call(
            attend_back_kernel,
            name="attend_back",
            grid=(clips,),
            in_specs=[smem(), by_clip(768)]
            + [one_clip(256)] * 4
            + [by_clip(128), by_clip(128), whole((frames_all, 1)), whole((1, frames_all))],
            out_specs=by_clip(768),
            out_shape=shaped((groups, clips, slab, 768), BF),
            compiler_params=params(),
            cost_estimate=cost(3, 2.0e9, 5e6),
        )(clip_lengths, sect, *mixed_grads, cosine, sine, fcol, frow)
        grad_proj = grad_proj.reshape(groups * rows, 768)
        return grad_proj

    def qkv_grad(act_one, grad_proj, packed, *sums):
        return pl.pallas_call(
            qkv_grad_kernel,
            name="qkv_grad",
            in_specs=[smem()] + [vmem()] * 6,
            out_shape=[
                shaped((144, 1024), BF),
                shaped((2, 144, 1024), BF),
                shaped((144, 1024), BF),
                shaped((4, 144, 1024), BF),
            ],
            scratch_shapes=[pltpu.VMEM((256, 768), F32), pltpu.VMEM((16, 1024), F32)],
            compiler_params=params(),
            cost_estimate=cost(3, 1.6e9, 6e6),
        )(ids, act_one.reshape(groups * rows, width), grad_proj, packed, *sums)

    def act_grad(grad_proj, weight_qkv, frame_slots):
        return pl.pallas_call(
            act_grad_kernel,
            name="act_grad",
            out_shape=[shaped((2, rows, width), BF)] * 2 + [shaped((8, width), F32)],
            compiler_params=params(),
            cost_estimate=cost(3, 1.6e9, 7e6),
        )(grad_proj, weight_qkv, *frame_slots)

    def mlp_out(hidden, seed_slots, mlp_pieces):
        return pl.pallas_call(
            functools.partial(mlp_out_kernel, depth),
            name="mlp_out",
            out_shape=[shaped((4, rows, width), BF)] * 2 + [shaped((8, width), F32)],
            scratch_shapes=[pltpu.VMEM((hidden_width, width), BF)],
            compiler_params=params(),
            cost_estimate=cost(4, 2.2e9, 11e6),
        )(*hidden, *seed_slots, mlp_pieces)

    def last(act_near, act_far, grad_resid, vecs):
        return pl.pallas_call(
            last_kernel,
            name="last",
            out_shape=shaped((rows, width), F32),
            compiler_params=params(),
            cost_estimate=cost(3, 8e6, 4e6),
        )(act_near, act_far, frames_flat, vecs, grad_resid).reshape(frames_in.shape)

    if rings:
        packet = begin()
        left, right, own_y, frame_x, frame_near, mlp_first = to_neighbours(packet)
        far, left_y, right_y, seed_x, out_left, out_right, frame_last, stats = further(left, right, frame_x, frame_near
        )
        frame_slots = [frames_flat, frame_near, frame_x, frame_last]
        mlp_pieces = lax.all_gather(after(mlp_first, far), "z", axis=0, tiled=True)
        weight_qkv, vecs, out_far = unpack([packet, own_y, left, left_y, right, right_y, far], out_left
        )
        outs = [w_out, out_left, out_right, out_far]
        (sect, act_one, mixed), outs, out_x, seed_y = attend_first(frame_slots, stats, weight_qkv, vecs, outs
        )
        (others, made), seed_corner = middle_first(mixed, outs, out_x, seed_x, vecs
        )
        mixed = [mixed[0], *others]
        weight_out, attn_out, resid, act_two = made
        seeds = [seeds_masked, seed_x, seed_y, seed_corner]
        others, seeds_near = share_act(act_two, seeds)
        act_slots = [act_two, *others]
        seed_slots = [seed for pair in zip(seeds, seeds_near) for seed in pair]
    else:
        mine = jnp.concatenate([v.reshape(1, piece_rows) for v in vectors], axis=1)
        vecs = lax.all_gather(mine, everywhere, axis=0, tiled=True).astype(F32)
        vecs = vecs.reshape(devices, 6, piece_rows).transpose(1, 0, 2).reshape(6, width)
        vecs = jnp.concatenate([vecs, jnp.zeros((2, width), F32)], axis=0)
        heads_in = w_qkv.reshape(piece_rows, 3, groups, 256).transpose(2, 0, 1, 3)
        heads_in = heads_in.reshape(groups, piece_rows, 768)
        heads_in = lax.all_to_all(heads_in, "seq", split_axis=0, concat_axis=0, tiled=True)
        heads_in = heads_in.reshape(groups * piece_rows, 768)
        weight_qkv = lax.all_gather(heads_in, ("z", "y"), axis=0, tiled=True)
        full = lax.all_gather(w_out, everywhere, axis=0, tiled=True)
        full = full.reshape(8, 4, 32, width)
        out_slots = [
            lax.dynamic_index_in_dim(full, s_here ^ m, 1, keepdims=False) for m in range(4)
        ]
        frame_slots = gather_seq(frames_flat)
        stats = norm_stats(frame_slots)
        wide_in = exchange_plane(wide_in)
        seed_slots = gather_plane(seeds_masked)
        sect, act_one, mixed = attend(frame_slots, stats, weight_qkv, vecs)
        others, made = middle(mixed, out_slots, vecs)
        mixed = [mixed[0], *others]
        weight_out, attn_out, resid, act_two = made
        act_slots = gather_plane(act_two)
        mlp_pieces = jnp.concatenate([wide_in, w_down], axis=0)
        mlp_pieces = lax.all_gather(mlp_pieces, "z", axis=0, tiled=True)
    hidden, back_parts, mlp_grads = mlp(act_slots, seed_slots, mlp_pieces, vecs)
    mlp_sums = lax.psum_scatter(mlp_grads, "z", scatter_dimension=0, tiled=True)
    back_parts = after(back_parts, mlp_grads)
    grad_resid, mixed_grads, even, odd, out_sums, middle_sums, scale_sums = middle_back(back_parts, resid, attn_out, vecs, weight_out, mixed, hidden, seed_slots, mlp_pieces,
    )
    wide_rows = 2 * groups * piece_rows
    if rings:
        halves = [added(even[k], odd[k]) for k in range(2)]
        grad_proj = attend_back(sect, mixed_grads)
        beside = over_seq(halves[1], 2)
        packed = added(after(halves[0], grad_proj), beside)
        out_far = over_seq(jnp.stack([out_sums[1], out_sums[3]]), 2)
        act_even, act_odd, norm_sums = act_grad(
            after(grad_proj, beside), weight_qkv, frame_slots
        )
        send_first, send_two, send_last, keep = qkv_grad(
            act_one, grad_proj, packed, norm_sums, middle_sums, scale_sums
        )
        act_odd = over_seq(act_odd, 1)
        act_near = added(act_even[0], act_odd[0])
        act_far = over_seq(added(act_even[1], act_odd[1]), 2)
        first = added(keep[0], over_y(send_first))
        two = over_y(after(send_two, first))
        out_near = out_sums[0].astype(F32) + out_far[0].astype(F32)
        out_side = added(out_sums[2], out_far[1])
        passed = over_z(after(first, mlp_sums, out_side), 1)
        blocks = [added(added(keep[1], two[0]), passed), added(keep[2], two[1])]
        send_last = over_y(after(send_last, two))
        out_side = over_y(after(out_side, two))
        left, right = over_z(blocks[0], 1), over_z(blocks[1], -1)
        input_grad = last(act_near, act_far, grad_resid, vecs)
        wide_out = exchange_plane(mlp_sums[:wide_rows].reshape(2 * groups, piece_rows, 1024))
        total = added(keep[3], send_last).astype(F32) + left.astype(F32) + right.astype(F32)
        total = after(total, input_grad, wide_out)
        parts = pl.pallas_call(
            prepare_kernel,
            name="prepare",
            out_shape=shaped((4, 48, 768), BF),
            compiler_params=params(),
            cost_estimate=cost(3, 1e6, 1e6),
        )(total)
        parts = lax.all_to_all(parts, "seq", split_axis=0, concat_axis=0, tiled=True)
        sum_qkv, sums = pl.pallas_call(
            finish_kernel,
            name="finish",
            out_shape=[shaped(w_qkv.shape, F32), shaped((8, 128), F32)],
            compiler_params=params(),
            cost_estimate=cost(3, 1e6, 1e6),
        )(parts)
        sums = sums[:, :piece_rows]
        sum_out = jnp.concatenate(
            [total[piece_rows * q : piece_rows * (q + 1), 768:] for q in range(4)], axis=1
        )
        mlp_result = out_near + out_side.astype(F32)
    else:
        packed = even[0]
        grad_proj = attend_back(sect, mixed_grads)
        act_even, act_odd, norm_sums = act_grad(grad_proj, weight_qkv, frame_slots)
        send_first, send_two, send_last, keep = qkv_grad(
            act_one, grad_proj, packed, norm_sums, middle_sums, scale_sums
        )
        act_odd = over_seq(act_odd, 1)
        act_near = added(act_even[0], act_odd[0])
        act_far = over_seq(added(act_even[1], act_odd[1]), 2)
        input_grad = last(act_near, act_far, grad_resid, vecs)
        sums = jnp.concatenate([norm_sums[0:2], middle_sums[0:3], scale_sums[0:1]], axis=0)
        sums = lax.psum(sums, everywhere)
        sums = lax.dynamic_index_in_dim(
            sums.reshape(6, devices, piece_rows), device, 1, keepdims=False
        )
        sends = jnp.concatenate([send_first[None], send_two, send_last[None]])
        full = jnp.stack([keep, sends], axis=1)[:, :, :128, :768].reshape(width, 768)
        sum_qkv = lax.psum_scatter(full, ("z", "y"), scatter_dimension=0, tiled=True)
        sum_qkv = sum_qkv.reshape(groups, piece_rows, 768)
        sum_qkv = lax.all_to_all(sum_qkv, "seq", split_axis=0, concat_axis=0, tiled=True)
        sum_qkv = sum_qkv.reshape(groups, piece_rows, 3, 256).transpose(1, 2, 0, 3)
        sum_qkv = sum_qkv.reshape(w_qkv.shape).astype(F32)
        full = jnp.stack([even[0], odd[0], even[1], odd[1]])
        full = jnp.stack(
            [lax.dynamic_index_in_dim(full, s_here ^ m, 0, keepdims=False) for m in range(4)], axis=1
        ).reshape(width, width)
        sum_out = lax.psum_scatter(full, everywhere, scatter_dimension=0, tiled=True).astype(F32)
        wide_out = exchange_plane(mlp_sums[:wide_rows].reshape(2 * groups, piece_rows, 1024))
        mlp_result = sum(part.astype(F32) for part in send_plane(out_sums))

    layer_out = (resid + mask * vecs[5:6, :] * mlp_result).astype(BF).reshape(frames_in.shape)
    wide_out = wide_out.reshape(2 * groups, piece_rows, 2, depth, units).transpose(1, 2, 3, 0, 4)
    sum_gate_up = wide_out.reshape(w_gate_up.shape).astype(F32)
    sum_down = mlp_sums[wide_rows:].astype(F32)

    return (
        layer_out,
        input_grad,
        sums[0],
        sums[1],
        sum_qkv,
        sum_out,
        sums[4],
        sums[2],
        sums[3],
        sum_gate_up,
        sum_down,
        sums[5],
    )


def solution(mesh):
    clip_groups, groups = mesh.shape["clips"], mesh.shape["seq"]
    depth = clip_groups // 2
    split = Mesh(mesh.devices.reshape(depth, 2, groups), ("z", "y", "seq"))
    clips, everywhere = ("z", "y"), ("z", "y", "seq")
    by_frame, by_clip = P(clips, "seq", None), P(clips)
    by_row, by_entry = P(everywhere, None), P(everywhere)
    return jax.shard_map(
        functools.partial(on_device, rings=depth == 4 and groups == 4),
        mesh=split,
        in_specs=(
            by_frame, by_frame, by_clip, by_clip, by_entry, by_entry, by_row, by_row,
            by_entry, by_entry, by_entry, by_row, by_row, by_entry,
        ),
        out_specs=(
            by_frame, by_frame, by_entry, by_entry, by_row, by_row, by_entry, by_entry,
            by_entry, by_row, by_row, by_entry,
        ),
        check_vma=False,
    )
```

```python
import functools

import jax
import jax.numpy as jnp
import numpy as np
from jax import lax
from jax.experimental import pallas as pl
from jax.experimental.pallas import tpu as pltpu
from jax.sharding import Mesh
from jax.sharding import PartitionSpec as P

H = 16
HD = 64
FF = 4096
WIN = 128
NEG_FILL = -1000000000.0
EPS = 1e-05
BF = jnp.bfloat16
F32 = jnp.float32
VMEM_BYTES = 56 * 1024 * 1024
COST_SCALE = (10, 10, 10, 10, 0.01)

ID_SEQ, ID_Y, ID_POS, ID_DEST, ID_CPOS = 0, 1, 2, 10, 14


def dot_nn(left, right):
    return jnp.dot(left, right, preferred_element_type=F32)


def dot_nt(left, right):
    return lax.dot_general(left, right, (((1,), (1,)), ((), ())), preferred_element_type=F32)


def dot_tn(left, right):
    return lax.dot_general(left, right, (((0,), (0,)), ((), ())), preferred_element_type=F32)


def smem():
    return pl.BlockSpec(memory_space=pltpu.SMEM)


def vmem():
    return pl.BlockSpec(memory_space=pltpu.VMEM)


def shaped(shape, dtype):
    return jax.ShapeDtypeStruct(shape, dtype)


def params():
    return pltpu.CompilerParams(vmem_limit_bytes=VMEM_BYTES)


def cost(phase, flops, moved):
    scale = COST_SCALE[phase]
    return pl.CostEstimate(
        flops=int(flops * scale), bytes_accessed=int(moved * scale), transcendentals=0
    )


def rows_at(index, size):
    return pl.ds(pl.multiple_of(index * size, size), size)


def normed(values):
    center = values - jnp.mean(values, axis=-1, keepdims=True)
    spread = lax.rsqrt(jnp.mean(center * center, axis=-1, keepdims=True) + EPS)
    return center * spread, spread


def pack_kernel(ids, weight, vector, *outs):
    me = ids[ID_SEQ]
    for slot, out in enumerate(outs):
        other = jnp.bitwise_xor(me, slot)
        for part in range(3):
            start = pl.multiple_of(part * 1024 + other * 256, 256)
            out[0:32, 256 * part : 256 * part + 256] = weight[:, pl.ds(start, 256)]
        out[32:48, 0:128] = vector[...]
        out[32:48, 128:768] = jnp.zeros((16, 640), BF)


def packet_kernel(s0, s1, s2, s3, packet):
    total = jnp.zeros((16, 128), F32)
    for slot, ref in enumerate((s0, s1, s2, s3)):
        packet[32 * slot : 32 * slot + 32, :] = ref[0:32, :]
        total = total + ref[32:48, 0:128].astype(F32)
    packet[128:144, 0:128] = total.astype(BF)
    packet[128:144, 128:768] = jnp.zeros((16, 640), BF)


def unpack_kernel(ids, *refs):
    pieces, (weight, vecs) = refs[:8], refs[8:]
    me = ids[ID_SEQ]
    for place, piece in enumerate(pieces):
        spot = ids[ID_POS + place]
        for slot in range(4):
            start = pl.multiple_of(spot * 128 + jnp.bitwise_xor(me, slot) * 32, 32)
            weight[pl.ds(start, 32), :] = piece[32 * slot : 32 * slot + 32, :]
        lanes = pl.ds(pl.multiple_of(spot * 128, 128), 128)
        vecs[:, lanes] = piece[128:144, 0:128].astype(F32)[0:8, :]


def norm_stats_kernel(x0, x1, x2, x3, mean, spread):
    for slot, frames in enumerate((x0, x1, x2, x3)):
        values = frames[...].astype(F32)
        middle = jnp.mean(values, axis=-1, keepdims=True)
        center = values - middle
        mean[slot] = middle
        spread[slot] = lax.rsqrt(jnp.mean(center * center, axis=-1, keepdims=True) + EPS)


def visible_bias(fcol, frow, length):
    gap = jnp.abs(fcol[...] - frow[...])
    seen = (gap <= WIN // 2) & (frow[...] < length.astype(F32))
    return jnp.where(seen, 0.0, NEG_FILL)


def turn(values, cosine, sine, lower):
    swapped = jnp.where(lower, pltpu.roll(values, 96, 1), pltpu.roll(values, 32, 1))
    return values * cosine + swapped * sine


def lane_masks():
    lane = lax.broadcasted_iota(jnp.int32, (1, 128), 1)
    lower = lane % 64 < 32
    return lower, [(lane // 64 == half).astype(F32) for half in (0, 1)]


def attend_kernel(
    lens, x0, x1, x2, x3, mean, spread, weight, vecs, cosine, sine, fcol, frow,
    sect, act, m0, m1, m2, m3,
):
    clip = pl.program_id(0)
    slab, width = x0.shape[1:]
    rows = 4 * slab
    frames = jnp.concatenate([x[0] for x in (x0, x1, x2, x3)], axis=0).astype(F32)
    frames = (frames - mean[...].reshape(rows, 1)) * spread[...].reshape(rows, 1)
    normal = (frames * vecs[0:1, :] + vecs[1:2, :]).astype(BF)
    act[...] = normal.reshape(act.shape)
    projected = dot_nn(normal, weight[...])
    cos_rows = cosine[...].reshape(rows, 128)
    sin_rows = sine[...].reshape(rows, 128)
    lower, masks = lane_masks()
    lower = jnp.broadcast_to(lower, (rows, 128))
    chunks = []
    for place in range(6):
        chunk = projected[:, 128 * place : 128 * place + 128]
        if place < 4:
            chunk = turn(chunk, cos_rows, sin_rows, lower)
        chunk = chunk.astype(BF)
        chunks.append(chunk)
        sect[:, 0, :, 128 * place : 128 * place + 128] = chunk.reshape(-1, slab, 128)
    bias = visible_bias(fcol, frow, lens[clip])
    for pair in range(2):
        total = jnp.zeros((rows, 128), F32)
        for half in range(2):
            mask = masks[half].astype(BF)
            scores = dot_nt(chunks[pair] * mask, chunks[2 + pair]) * HD ** (-0.5) + bias
            expo = jnp.exp(scores - jnp.max(scores, axis=-1, keepdims=True))
            weights = (expo * (1.0 / jnp.sum(expo, axis=-1, keepdims=True))).astype(BF)
            total = total + dot_nn(weights, chunks[4 + pair] * mask)
        total = total.astype(BF)
        for slot, out in enumerate((m0, m1, m2, m3)):
            out[0, :, 128 * pair : 128 * pair + 128] = total[slab * slot : slab * (slot + 1)]


def attend_back_kernel(lens, sect, g0, g1, g2, g3, cosine, sine, fcol, frow, grad):
    clip = pl.program_id(0)
    slab = sect.shape[2]
    rows = sect.shape[0] * slab
    cos_rows = cosine[...].reshape(rows, 128)
    sin_rows = -sine[...].reshape(rows, 128)
    lower, masks = lane_masks()
    lower = jnp.broadcast_to(lower, (rows, 128))
    bias = visible_bias(fcol, frow, lens[clip])

    def part(place):
        return sect[:, 0, :, 128 * place : 128 * place + 128].reshape(rows, 128)

    def put(place, values):
        grad[:, 0, :, 128 * place : 128 * place + 128] = values.astype(BF).reshape(-1, slab, 128)

    for pair in range(2):
        queries, keys_in, values_in = part(pair), part(2 + pair), part(4 + pair)
        mixed_grad = jnp.concatenate(
            [g[0, :, 128 * pair : 128 * pair + 128] for g in (g0, g1, g2, g3)], axis=0
        )
        grad_q = jnp.zeros((rows, 128), F32)
        grad_k = jnp.zeros((rows, 128), F32)
        grad_v = jnp.zeros((rows, 128), F32)
        for half in range(2):
            mask = masks[half].astype(BF)
            query = queries * mask
            upper = mixed_grad * mask
            scores = dot_nt(query, keys_in) * HD ** (-0.5) + bias
            expo = jnp.exp(scores - jnp.max(scores, axis=-1, keepdims=True))
            probs = expo * (1.0 / jnp.sum(expo, axis=-1, keepdims=True))
            grad_v = grad_v + dot_tn(probs.astype(BF), upper)
            grad_probs = dot_nt(upper, values_in)
            centre = jnp.sum(probs * grad_probs, axis=-1, keepdims=True)
            grad_scores = (probs * (grad_probs - centre)).astype(BF)
            grad_q = grad_q + dot_nn(grad_scores, keys_in * mask)
            grad_k = grad_k + dot_tn(grad_scores, query)
        grad_q = (grad_q * HD ** (-0.5)).astype(BF).astype(F32)
        grad_k = (grad_k * HD ** (-0.5)).astype(BF).astype(F32)
        put(pair, turn(grad_q, cos_rows, sin_rows, lower))
        put(2 + pair, turn(grad_k, cos_rows, sin_rows, lower))
        put(4 + pair, grad_v)


def middle_kernel(
    ids, m0, m1, m2, m3, w0, w1, w2, w3, frames, mask, vecs, weight, attn_out, resid, act
):
    me = ids[ID_SEQ]
    for slot, packed in enumerate((w0, w1, w2, w3)):
        other = jnp.bitwise_xor(me, slot)
        for place in range(8):
            start = pl.multiple_of(ids[ID_POS + place] * 128 + other * 32, 32)
            weight[pl.ds(start, 32), :] = packed[place]
    total = jnp.zeros(attn_out.shape, F32)
    for slot, mixed in enumerate((m0, m1, m2, m3)):
        block = weight[rows_at(jnp.bitwise_xor(me, slot), 256), :]
        total = total + dot_nn(mixed[...], block)
    attn_out[...] = total
    summed = frames[...].astype(F32) + mask[...] * vecs[2:3, :] * total
    resid[...] = summed
    xhat, _ = normed(summed)
    act[...] = (xhat * vecs[3:4, :] + vecs[4:5, :]).astype(BF)


def middle_back_kernel(
    ids, q0, q1, q2, q3, resid, attn_out, grad_in, mask, vecs, weight,
    grad_resid, grad_attn, g0, g1, g2, g3, sums,
):
    me = ids[ID_SEQ]
    grad_act = q0[...].astype(F32) + q1[...].astype(F32) + q2[...].astype(F32) + q3[...].astype(F32)
    xhat, spread = normed(resid[...])
    sums[0:1, :] = jnp.sum(grad_act * xhat, axis=0, keepdims=True)
    sums[1:2, :] = jnp.sum(grad_act, axis=0, keepdims=True)
    pulled = grad_act * vecs[3:4, :]
    pulled = spread * (
        pulled
        - jnp.mean(pulled, axis=-1, keepdims=True)
        - xhat * jnp.mean(pulled * xhat, axis=-1, keepdims=True)
    )
    total = grad_in[...].astype(F32) + pulled
    grad_resid[...] = total
    masked = mask[...] * total
    sums[2:3, :] = jnp.sum(masked * attn_out[...], axis=0, keepdims=True)
    sums[3:8, :] = jnp.zeros((5, sums.shape[1]), F32)
    scaled = (masked * vecs[2:3, :]).astype(BF)
    grad_attn[...] = scaled
    for slot, out in enumerate((g0, g1, g2, g3)):
        block = weight[rows_at(jnp.bitwise_xor(me, slot), 256), :]
        out[...] = dot_nt(scaled, block).astype(BF)


def out_grad_kernel(ids, m0, m1, m2, m3, grad_attn, even, odd, held):
    me = ids[ID_SEQ]
    for slot, mixed in enumerate((m0, m1, m2, m3)):
        held[rows_at(jnp.bitwise_xor(me, slot), 256), :] = dot_tn(mixed[...], grad_attn[...]).astype(
            BF
        )
    for slot in range(4):
        other = jnp.bitwise_xor(me, slot)
        out = odd if slot % 2 else even
        for place in range(8):
            start = pl.multiple_of(ids[ID_CPOS + place] * 128 + other * 32, 32)
            out[slot // 2, place] = held[pl.ds(start, 32), :]


def piece_parts(depth, held, place):
    wide, down = 1024 // depth, held // depth
    start = (wide + down) * place
    return (
        (slice(start, start + wide), slice(wide * place, wide * place + wide)),
        (slice(start + wide, start + wide + down), slice(down * place, down * place + down)),
    )


def spread_pieces(depth, pieces, w_in, w_down):
    for place in range(depth):
        upper, lower = piece_parts(depth, w_down.shape[0], place)
        if w_in is not None:
            w_in[upper[1], :] = pieces[upper[0], :]
        w_down[lower[1], :] = pieces[lower[0], :]


def mlp_kernel(
    depth, a0, a1, o0, o1, pieces, vecs, hidden, grads, grad_mlp, even, odd, w_in, w_down
):
    spread_pieces(depth, pieces, w_in, w_down)
    width = hidden.shape[1]
    for slot, (act, seed, out) in enumerate(((a0, o0, even), (a1, o1, odd))):
        here = slice(256 * slot, 256 * slot + 256)
        gate_up = dot_nn(act[...], w_in[...])
        gate, up = gate_up[:, :width], gate_up[:, width:]
        pulled = (vecs[5:6, :] * seed[...].astype(F32)).astype(BF)
        grad_mlp[here, :] = pulled
        grad_hidden = dot_nt(pulled, w_down[...])
        sig = jax.nn.sigmoid(gate)
        silu = gate * sig
        hidden[here, :] = (silu * up).astype(BF)
        grad_gate = grad_hidden * up * sig * (1.0 + gate * (1.0 - sig))
        grads[here, :width] = grad_gate.astype(BF)
        grads[here, width:] = (grad_hidden * silu).astype(BF)
        out[...] = dot_nt(grads[here, :], w_in[...]).astype(BF)


def started(copies):
    for copy in copies:
        copy.start()
    return copies


def mlp_grad_kernel(depth, *refs):
    acts, refs = refs[:8], refs[8:]
    grads, hidden, grad_mlp, out, refs = refs[0:4], refs[4:8], refs[8:12], refs[12], refs[13:]
    act_v, grads_v, hidden_v, grad_mlp_v, upper, lower, upper_out, lower_out, in_sems, out_sems = refs
    arrivals = []
    for chunk in range(4):
        here = pl.ds(512 * chunk, 512)
        pairs = [
            (acts[2 * chunk], act_v.at[pl.ds(512 * chunk, 256)]),
            (acts[2 * chunk + 1], act_v.at[pl.ds(512 * chunk + 256, 256)]),
            (grads[chunk], grads_v.at[here]),
            (hidden[chunk], hidden_v.at[here]),
            (grad_mlp[chunk], grad_mlp_v.at[here]),
        ]
        arrivals.append(
            started(
                [
                    pltpu.make_async_copy(source, held, in_sems.at[5 * chunk + at])
                    for at, (source, held) in enumerate(pairs)
                ]
            )
        )
    leaving = []
    for chunk in range(4):
        for copy in arrivals[chunk]:
            copy.wait()
        here = slice(512 * chunk, 512 * chunk + 512)
        for block in range(4):
            wide = slice(256 * block, 256 * block + 256)
            narrow = slice(128 * block, 128 * block + 128)
            total = dot_tn(act_v[here, wide], grads_v[here, :])
            rest = dot_tn(hidden_v[here, narrow], grad_mlp_v[here, :])
            if chunk > 0:
                total = total + upper[wide, :]
                rest = rest + lower[narrow, :]
            if chunk < 3:
                upper[wide, :] = total
                lower[narrow, :] = rest
                continue
            upper_out[wide, :] = total.astype(BF)
            lower_out[narrow, :] = rest.astype(BF)
            for place in range(depth * block // 4, depth * (block + 1) // 4):
                first, second = piece_parts(depth, lower_out.shape[0], place)
                leaving += started(
                    [
                        pltpu.make_async_copy(
                            upper_out.at[first[1]], out.at[first[0]], out_sems.at[2 * place]
                        ),
                        pltpu.make_async_copy(
                            lower_out.at[second[1]], out.at[second[0]], out_sems.at[2 * place + 1]
                        ),
                    ]
                )
    for copy in leaving:
        copy.wait()


def mlp_out_kernel(depth, *refs):
    hidden, refs = refs[:4], refs[4:]
    seeds, refs = refs[:8], refs[8:]
    pieces, refs = refs[0], refs[1:]
    even, odd, sums, w_down = refs
    spread_pieces(depth, pieces, None, w_down)
    total = jnp.zeros((1, sums.shape[1]), F32)
    for slot in range(8):
        here = slice(256 * (slot % 2), 256 * (slot % 2) + 256)
        result = dot_nn(hidden[slot // 2][here, :], w_down[...])
        out = odd if slot % 2 else even
        out[slot // 2] = result.astype(BF)
        total = total + jnp.sum(result * seeds[slot][...].astype(F32), axis=0, keepdims=True)
    sums[...] = jnp.concatenate([total, jnp.zeros((7, sums.shape[1]), F32)], axis=0)


def qkv_grad_kernel(
    ids, act, grad, packed, norm_sums, middle_sums, scale_sums, send_first, send_two, send_last, keep, held, sums
):
    sums[0:8, :] = jnp.concatenate(
        [norm_sums[0:2, :], middle_sums[0:3, :], scale_sums[0:1, :], jnp.zeros((2, 1024), F32)],
        axis=0,
    )
    sums[8:16, :] = jnp.zeros((8, 1024), F32)
    y_here = ids[ID_Y]
    for place in range(4):
        block = ids[ID_DEST + place]
        wide = pl.ds(pl.multiple_of(block * 256, 256), 256)
        held[...] = dot_tn(act[:, wide], grad[...])
        send = (send_first, send_two.at[0], send_two.at[1], send_last)[place]
        for half, out in ((0, keep.at[place]), (1, send)):
            row = y_here if half == 0 else 1 - y_here
            out[0:128, 0:768] = held[rows_at(row, 128), :].astype(BF)
            for quarter in range(4):
                out[32 * quarter : 32 * quarter + 32, 768:1024] = packed[
                    2 * place + half, :, 256 * quarter : 256 * quarter + 256
                ]
            lanes = pl.ds(pl.multiple_of(block * 256 + row * 128, 128), 128)
            out[128:144, 0:128] = sums[:, lanes].astype(BF)
            out[128:144, 128:1024] = jnp.zeros((16, 896), BF)


def prepare_kernel(total, parts):
    for place in range(4):
        parts[place, 0:32, :] = total[32 * place : 32 * place + 32, 0:768].astype(BF)
        block = total[128:144, 0:128]
        block = pltpu.roll(block, 128 - 32 * place, 1) if place else block
        parts[place, 32:48, 0:128] = block.astype(BF)
        parts[place, 32:48, 128:768] = jnp.zeros((16, 640), BF)


def finish_kernel(parts, out, sums):
    total = jnp.zeros((16, 128), F32)
    for place in range(4):
        for part in range(3):
            start = 1024 * part + 256 * place
            here = 256 * part
            out[:, start : start + 256] = parts[place, 0:32, here : here + 256].astype(F32)
        total = total + parts[place, 32:48, 0:128].astype(F32)
    sums[...] = total[0:8, :]


def act_grad_kernel(grad, weight, x0, x1, x2, x3, even, odd, sums):
    gain_sum = jnp.zeros((1, sums.shape[1]), F32)
    bias_sum = jnp.zeros((1, sums.shape[1]), F32)
    for slot, frames in enumerate((x0, x1, x2, x3)):
        result = dot_nt(grad[256 * slot : 256 * slot + 256, :], weight[...])
        out = odd if slot % 2 else even
        out[slot // 2] = result.astype(BF)
        xhat, _ = normed(frames[...].astype(F32))
        gain_sum = gain_sum + jnp.sum(result * xhat, axis=0, keepdims=True)
        bias_sum = bias_sum + jnp.sum(result, axis=0, keepdims=True)
    sums[...] = jnp.concatenate(
        [gain_sum, bias_sum, jnp.zeros((6, sums.shape[1]), F32)], axis=0
    )


def last_kernel(u, v, frames, vecs, grad_resid, out):
    grad_act = u[...].astype(F32) + v[...].astype(F32)
    xhat, spread = normed(frames[...].astype(F32))
    pulled = grad_act * vecs[0:1, :]
    out[...] = grad_resid[...] + spread * (
        pulled
        - jnp.mean(pulled, axis=-1, keepdims=True)
        - xhat * jnp.mean(pulled * xhat, axis=-1, keepdims=True)
    )


def added(left, right):
    return (left.astype(F32) + right.astype(F32)).astype(BF)


def after(value, *first):
    return lax.optimization_barrier((value, first))[0]


def on_device(
    frames_in,
    output_grad,
    clip_kinds,
    clip_lengths,
    norm1_gain,
    norm1_bias,
    w_qkv,
    w_out,
    attn_scale,
    norm2_gain,
    norm2_bias,
    w_gate_up,
    w_down,
    mlp_scale,
    *,
    rings,
):
    depth = lax.axis_size("z")
    groups = lax.axis_size("seq")
    z_here, y_here, s_here = lax.axis_index("z"), lax.axis_index("y"), lax.axis_index("seq")
    everywhere = ("z", "y", "seq")
    plane = ("y", "seq")
    clips, slab, width = frames_in.shape
    rows = clips * slab
    device = (z_here * 2 + y_here) * groups + s_here
    devices = depth * 2 * groups
    piece_rows = w_qkv.shape[0]

    def over_seq(array_in, flip):
        return lax.ppermute(array_in, "seq", [(i, i ^ flip) for i in range(groups)])

    def over_y(array_in):
        return lax.ppermute(array_in, "y", [(0, 1), (1, 0)])

    def over_corner(array_in):
        pairs = [
            (y * groups + s, (1 - y) * groups + (s ^ 2)) for y in range(2) for s in range(groups)
        ]
        return lax.ppermute(array_in, plane, pairs)

    def over_z(array_in, step):
        return lax.ppermute(array_in, "z", [(i, (i + step) % depth) for i in range(depth)])

    def gather_z(array_in):
        left, right = over_z(array_in, 1), over_z(array_in, -1)
        return [array_in, left, right, over_z(left, 1)]

    def scatter_z(blocks):
        passed = added(blocks[1], over_z(blocks[0], 1))
        left, right = over_z(passed, 1), over_z(blocks[2], -1)
        return blocks[3].astype(F32) + left.astype(F32) + right.astype(F32)

    def gather_seq(array_in):
        near, far = over_seq(array_in, 1), over_seq(array_in, 2)
        return [array_in, near, far, over_seq(far, 1)]

    def gather_plane(array_in):
        slots = [array_in, over_seq(array_in, 1)]
        beside, across = over_seq(array_in, 2), over_y(array_in)
        for arrived in (beside, across, over_corner(array_in)):
            slots += [arrived, over_seq(arrived, 1)]
        return slots

    def scatter_plane(slots):
        return send_plane(
            [added(slots[2 * p], over_seq(slots[2 * p + 1], 1)) for p in range(4)]
        )

    def send_plane(sums):
        return [sums[0], over_seq(sums[1], 2), over_y(sums[2]), over_corner(sums[3])]

    def exchange_plane(array_in):
        parts = lax.all_to_all(array_in, plane, split_axis=0, concat_axis=0, tiled=True)
        return parts.reshape(-1, array_in.shape[-1])

    def norm_stats(slots):
        return pl.pallas_call(
            norm_stats_kernel,
            name="norm_stats",
            out_shape=[shaped((groups, rows, 1), F32)] * 2,
            compiler_params=params(),
            cost_estimate=cost(0, 16e6, 6e6),
        )(*slots)

    if rings:
        came = [(z_here + k) % depth for k in (0, -1, 1, -2)]
        dest = [(z_here + k) % depth for k in (2, 1, -1, 0)]
        pos = [came[k] * 2 + (y_here if h == 0 else 1 - y_here) for k in range(4) for h in (0, 1)]
        y_row = y_here
    else:
        dest = [jnp.int32(k) for k in range(4)]
        pos = [jnp.int32(k) for k in range(8)]
        y_row = jnp.int32(0)
    cpos = [dest[k] * 2 + (y_row if h == 0 else 1 - y_row) for k in range(4) for h in (0, 1)]
    ids = jnp.stack([s_here, y_row, *pos, *dest, *cpos]).astype(jnp.int32)

    frame_times = s_here * slab + jnp.arange(slab)
    mask = (frame_times[None, :] < clip_lengths[:, None]).astype(F32).reshape(rows, 1)
    slot_times = (
        (jnp.arange(groups) ^ s_here)[:, None] * slab + jnp.arange(slab)[None, :]
    ).astype(F32)
    rates = 1.0 + clip_kinds.astype(F32)
    positions = slot_times[:, None, :] * rates[None, :, None]
    lane = jnp.arange(128)
    inv_freq = 10000.0 ** (-2.0 * (lane % 32).astype(F32) / HD)
    angles = positions[..., None] * inv_freq
    cosine = jnp.cos(angles)
    sine = jnp.sin(angles) * jnp.where(lane % 64 < 32, -1.0, 1.0)
    fcol = slot_times.reshape(groups * slab, 1)
    frow = slot_times.reshape(1, groups * slab)

    frames_flat = frames_in.reshape(rows, width)
    seeds_flat = output_grad.reshape(rows, width)
    seeds_masked = (seeds_flat.astype(F32) * mask).astype(BF)
    vectors = (norm1_gain, norm1_bias, attn_scale, norm2_gain, norm2_bias, mlp_scale)
    units = w_down.shape[0]
    hidden_width = FF // (2 * groups)
    frames_all = groups * slab
    wide_in = w_gate_up.reshape(piece_rows, 2, depth, 2 * groups, units).transpose(3, 0, 1, 2, 4)
    wide_in = wide_in.reshape(2 * groups, piece_rows, 1024)

    def by_clip(last):
        return pl.BlockSpec((groups, 1, slab, last), lambda c: (0, c, 0, 0))

    def one_clip(last):
        return pl.BlockSpec((1, slab, last), lambda c: (c, 0, 0))

    def whole(shape):
        return pl.BlockSpec(shape, lambda c: (0,) * len(shape))

    def begin():
        mine = jnp.pad(jnp.stack(vectors), ((0, 10), (0, 96)))
        mine = jnp.roll(mine, s_here * 32, axis=1)
        slots = pl.pallas_call(
            pack_kernel,
            name="pack",
            in_specs=[smem(), vmem(), vmem()],
            out_shape=[shaped((48, 768), BF)] * 4,
            compiler_params=params(),
            cost_estimate=cost(0, 1e6, 5e5),
        )(ids, w_qkv, mine)
        slots = [slots[0]] + [over_seq(slots[m], m) for m in (2, 3, 1)]
        packet = pl.pallas_call(
            packet_kernel,
            name="packet",
            out_shape=shaped((144, 768), BF),
            compiler_params=params(),
            cost_estimate=cost(0, 1e6, 8e5),
        )(*after((slots[0], slots[3], slots[1], slots[2]), cosine, sine, fcol, frow))
        return packet

    def to_neighbours(packet):
        wide = exchange_plane(wide_in)
        return (
            over_z(packet, 1),
            over_z(packet, -1),
            over_y(packet),
            over_seq(frames_flat, 2),
            over_seq(frames_flat, 1),
            jnp.concatenate([wide, w_down], axis=0),
        )

    def further(left, right, frame_x, frame_near):
        frame_last = over_seq(frame_x, 1)
        return (
            over_z(left, 1),
            over_y(left),
            over_y(right),
            over_seq(seeds_masked, 2),
            over_z(w_out, 1),
            over_z(w_out, -1),
            frame_last,
            norm_stats([frames_flat, frame_near, frame_x, frame_last]),
        )

    def unpack(pieces, out):
        last_y = over_y(pieces[-1])
        out_last = over_z(out, 1)
        weight_qkv, vecs = pl.pallas_call(
            unpack_kernel,
            name="unpack",
            in_specs=[smem()] + [vmem()] * 8,
            out_shape=[shaped((width, 768), BF), shaped((8, width), F32)],
            compiler_params=params(),
            cost_estimate=cost(1, 1e6, 4e6),
        )(ids, *pieces, last_y)
        return weight_qkv, vecs, out_last

    def attend(frame_slots, stats, weight_qkv, vecs):
        frame_slots = [slot.reshape(clips, slab, width) for slot in frame_slots]
        stats = [stat.reshape(groups, clips, slab, 1) for stat in stats]
        sect, act_one, *mixed = pl.pallas_call(
            attend_kernel,
            name="attend",
            grid=(clips,),
            in_specs=[smem()]
            + [one_clip(width)] * 4
            + [by_clip(1), by_clip(1), whole((width, 768)), whole((8, width))]
            + [by_clip(128), by_clip(128), whole((frames_all, 1)), whole((1, frames_all))],
            out_specs=[by_clip(768), by_clip(width)] + [one_clip(256)] * 4,
            out_shape=[
                shaped((groups, clips, slab, 768), BF),
                shaped((groups, clips, slab, width), BF),
            ]
            + [shaped((clips, slab, 256), BF)] * 4,
            compiler_params=params(),
            cost_estimate=cost(1, 2.4e9, 8e6),
        )(clip_lengths, *frame_slots, *stats, weight_qkv, vecs, cosine, sine, fcol, frow)
        return sect, act_one, [m.reshape(rows, 256) for m in mixed]

    def attend_first(frame_slots, stats, weight_qkv, vecs, outs):
        outs = jnp.stack(outs)
        outs = jnp.stack([outs, over_y(outs)], axis=1).reshape(8, piece_rows, width)
        made = attend(frame_slots, stats, weight_qkv, vecs)
        return made, outs, over_seq(outs, 2), over_y(seeds_masked)

    def middle(mixed, out_slots, vecs):
        mixed = [over_seq(mixed[m], m) if m else mixed[0] for m in range(4)]
        made = pl.pallas_call(
            middle_kernel,
            name="middle",
            in_specs=[smem()] + [vmem()] * 11,
            out_shape=[
                shaped((width, width), BF),
                shaped((rows, width), F32),
                shaped((rows, width), F32),
                shaped((rows, width), BF),
            ],
            compiler_params=params(),
            cost_estimate=cost(1, 0.6e9, 9e6),
        )(ids, *mixed, *out_slots, frames_flat, mask, vecs)
        return mixed[1:], made

    def middle_first(mixed, outs, out_x, seed_x, vecs):
        out_slots = [outs, over_seq(outs, 1), out_x, over_seq(out_x, 1)]
        return middle(mixed, out_slots, vecs), over_y(seed_x)

    def share_act(act_two, seeds):
        return gather_plane(act_two)[1:], [over_seq(seed, 1) for seed in seeds]

    def mlp(act_slots, seed_slots, mlp_pieces, vecs):
        pair_out = [None] * 4
        sums = [None] * 4
        order = (3, 1, 2, 0)
        for turn_at, pair in enumerate(order):
            acts = act_slots[2 * pair : 2 * pair + 2]
            if turn_at > 1:
                acts = after(acts, sums[order[turn_at - 2]])
            pair_out[pair] = pl.pallas_call(
                functools.partial(mlp_kernel, depth),
                name="mlp",
                out_shape=[
                    shaped((2 * rows, hidden_width), BF),
                    shaped((2 * rows, 2 * hidden_width), BF),
                    shaped((2 * rows, width), BF),
                    shaped((rows, width), BF),
                    shaped((rows, width), BF),
                ],
                scratch_shapes=[
                    pltpu.VMEM((width, 2 * hidden_width), BF),
                    pltpu.VMEM((hidden_width, width), BF),
                ],
                compiler_params=params(),
                cost_estimate=cost(2, 3.2e9, 10e6),
            )(*acts, *seed_slots[2 * pair : 2 * pair + 2], mlp_pieces, vecs)
            sums[pair] = added(pair_out[pair][3], over_seq(pair_out[pair][4], 1))
        hidden = [p[0] for p in pair_out]
        back_parts = send_plane(sums)
        mlp_grads = pl.pallas_call(
            functools.partial(mlp_grad_kernel, depth),
            name="mlp_grad",
            in_specs=[pl.BlockSpec(memory_space=pl.ANY)] * 20,
            out_specs=pl.BlockSpec(memory_space=pl.ANY),
            out_shape=shaped((width + hidden_width, width), BF),
            scratch_shapes=[
                pltpu.VMEM((8 * rows, width), BF),
                pltpu.VMEM((8 * rows, 2 * hidden_width), BF),
                pltpu.VMEM((8 * rows, hidden_width), BF),
                pltpu.VMEM((8 * rows, width), BF),
                pltpu.VMEM((width, width), F32),
                pltpu.VMEM((hidden_width, width), F32),
                pltpu.VMEM((width, width), BF),
                pltpu.VMEM((hidden_width, width), BF),
                pltpu.SemaphoreType.DMA((20,)),
                pltpu.SemaphoreType.DMA((2 * depth,)),
            ],
            compiler_params=params(),
            cost_estimate=cost(2, 6.4e9, 17e6),
        )(*act_slots, *[p[1] for p in pair_out], *hidden, *[p[2] for p in pair_out])
        return hidden, back_parts, mlp_grads

    def middle_back(back_parts, resid, attn_out, vecs, weight_out, mixed, *rest):
        grad_resid, grad_attn, *mixed_grads, middle_sums = pl.pallas_call(
            middle_back_kernel,
            name="middle_back",
            in_specs=[smem()] + [vmem()] * 10,
            out_shape=[shaped((rows, width), F32), shaped((rows, width), BF)]
            + [shaped((rows, 256), BF)] * 4
            + [shaped((8, width), F32)],
            compiler_params=params(),
            cost_estimate=cost(3, 0.6e9, 9e6),
        )(ids, *back_parts, resid, attn_out, seeds_flat, mask, vecs, weight_out)
        mixed_grads = [over_seq(g, m) if m else g for m, g in enumerate(mixed_grads)]
        out_even, out_odd, scale_sums = mlp_out(*after(rest, grad_attn))
        out_odd = over_seq(out_odd, 1)
        even, odd = pl.pallas_call(
            out_grad_kernel,
            name="out_grad",
            in_specs=[smem()] + [vmem()] * 5,
            out_shape=[shaped((2, 8, 32, width), BF)] * 2,
            scratch_shapes=[pltpu.VMEM((width, width), BF)],
            compiler_params=params(),
            cost_estimate=cost(4, 0.6e9, 4e6),
        )(ids, *after(mixed, scale_sums), grad_attn)
        odd = over_seq(odd, 1) if rings else odd
        out_sums = [added(out_even[k], out_odd[k]) for k in range(4)]
        return grad_resid, mixed_grads, even, odd, out_sums, middle_sums, scale_sums

    def attend_back(sect, mixed_grads):
        mixed_grads = [g.reshape(clips, slab, 256) for g in mixed_grads]
        grad_proj = pl.pallas_call(
            attend_back_kernel,
            name="attend_back",
            grid=(clips,),
            in_specs=[smem(), by_clip(768)]
            + [one_clip(256)] * 4
            + [by_clip(128), by_clip(128), whole((frames_all, 1)), whole((1, frames_all))],
            out_specs=by_clip(768),
            out_shape=shaped((groups, clips, slab, 768), BF),
            compiler_params=params(),
            cost_estimate=cost(3, 2.0e9, 5e6),
        )(clip_lengths, sect, *mixed_grads, cosine, sine, fcol, frow)
        grad_proj = grad_proj.reshape(groups * rows, 768)
        return grad_proj

    def qkv_grad(act_one, grad_proj, packed, *sums):
        return pl.pallas_call(
            qkv_grad_kernel,
            name="qkv_grad",
            in_specs=[smem()] + [vmem()] * 6,
            out_shape=[
                shaped((144, 1024), BF),
                shaped((2, 144, 1024), BF),
                shaped((144, 1024), BF),
                shaped((4, 144, 1024), BF),
            ],
            scratch_shapes=[pltpu.VMEM((256, 768), F32), pltpu.VMEM((16, 1024), F32)],
            compiler_params=params(),
            cost_estimate=cost(3, 1.6e9, 6e6),
        )(ids, act_one.reshape(groups * rows, width), grad_proj, packed, *sums)

    def act_grad(grad_proj, weight_qkv, frame_slots):
        return pl.pallas_call(
            act_grad_kernel,
            name="act_grad",
            out_shape=[shaped((2, rows, width), BF)] * 2 + [shaped((8, width), F32)],
            compiler_params=params(),
            cost_estimate=cost(3, 1.6e9, 7e6),
        )(grad_proj, weight_qkv, *frame_slots)

    def mlp_out(hidden, seed_slots, mlp_pieces):
        return pl.pallas_call(
            functools.partial(mlp_out_kernel, depth),
            name="mlp_out",
            out_shape=[shaped((4, rows, width), BF)] * 2 + [shaped((8, width), F32)],
            scratch_shapes=[pltpu.VMEM((hidden_width, width), BF)],
            compiler_params=params(),
            cost_estimate=cost(4, 2.2e9, 11e6),
        )(*hidden, *seed_slots, mlp_pieces)

    def last(act_near, act_far, grad_resid, vecs):
        return pl.pallas_call(
            last_kernel,
            name="last",
            out_shape=shaped((rows, width), F32),
            compiler_params=params(),
            cost_estimate=cost(3, 8e6, 4e6),
        )(act_near, act_far, frames_flat, vecs, grad_resid).reshape(frames_in.shape)

    if rings:
        packet = begin()
        left, right, own_y, frame_x, frame_near, mlp_first = to_neighbours(packet)
        far, left_y, right_y, seed_x, out_left, out_right, frame_last, stats = further(left, right, frame_x, frame_near
        )
        frame_slots = [frames_flat, frame_near, frame_x, frame_last]
        mlp_pieces = lax.all_gather(after(mlp_first, far), "z", axis=0, tiled=True)
        weight_qkv, vecs, out_far = unpack([packet, own_y, left, left_y, right, right_y, far], out_left
        )
        outs = [w_out, out_left, out_right, out_far]
        (sect, act_one, mixed), outs, out_x, seed_y = attend_first(frame_slots, stats, weight_qkv, vecs, outs
        )
        (others, made), seed_corner = middle_first(mixed, outs, out_x, seed_x, vecs
        )
        mixed = [mixed[0], *others]
        weight_out, attn_out, resid, act_two = made
        seeds = [seeds_masked, seed_x, seed_y, seed_corner]
        others, seeds_near = share_act(act_two, seeds)
        act_slots = [act_two, *others]
        seed_slots = [seed for pair in zip(seeds, seeds_near) for seed in pair]
    else:
        mine = jnp.concatenate([v.reshape(1, piece_rows) for v in vectors], axis=1)
        vecs = lax.all_gather(mine, everywhere, axis=0, tiled=True).astype(F32)
        vecs = vecs.reshape(devices, 6, piece_rows).transpose(1, 0, 2).reshape(6, width)
        vecs = jnp.concatenate([vecs, jnp.zeros((2, width), F32)], axis=0)
        heads_in = w_qkv.reshape(piece_rows, 3, groups, 256).transpose(2, 0, 1, 3)
        heads_in = heads_in.reshape(groups, piece_rows, 768)
        heads_in = lax.all_to_all(heads_in, "seq", split_axis=0, concat_axis=0, tiled=True)
        heads_in = heads_in.reshape(groups * piece_rows, 768)
        weight_qkv = lax.all_gather(heads_in, ("z", "y"), axis=0, tiled=True)
        full = lax.all_gather(w_out, everywhere, axis=0, tiled=True)
        full = full.reshape(8, 4, 32, width)
        out_slots = [
            lax.dynamic_index_in_dim(full, s_here ^ m, 1, keepdims=False) for m in range(4)
        ]
        frame_slots = gather_seq(frames_flat)
        stats = norm_stats(frame_slots)
        wide_in = exchange_plane(wide_in)
        seed_slots = gather_plane(seeds_masked)
        sect, act_one, mixed = attend(frame_slots, stats, weight_qkv, vecs)
        others, made = middle(mixed, out_slots, vecs)
        mixed = [mixed[0], *others]
        weight_out, attn_out, resid, act_two = made
        act_slots = gather_plane(act_two)
        mlp_pieces = jnp.concatenate([wide_in, w_down], axis=0)
        mlp_pieces = lax.all_gather(mlp_pieces, "z", axis=0, tiled=True)
    hidden, back_parts, mlp_grads = mlp(act_slots, seed_slots, mlp_pieces, vecs)
    mlp_sums = lax.psum_scatter(mlp_grads, "z", scatter_dimension=0, tiled=True)
    back_parts = after(back_parts, mlp_grads)
    grad_resid, mixed_grads, even, odd, out_sums, middle_sums, scale_sums = middle_back(back_parts, resid, attn_out, vecs, weight_out, mixed, hidden, seed_slots, mlp_pieces,
    )
    wide_rows = 2 * groups * piece_rows
    if rings:
        halves = [added(even[k], odd[k]) for k in range(2)]
        grad_proj = attend_back(sect, mixed_grads)
        beside = over_seq(halves[1], 2)
        packed = added(after(halves[0], grad_proj), beside)
        out_far = over_seq(jnp.stack([out_sums[1], out_sums[3]]), 2)
        act_even, act_odd, norm_sums = act_grad(
            after(grad_proj, beside), weight_qkv, frame_slots
        )
        send_first, send_two, send_last, keep = qkv_grad(
            act_one, grad_proj, packed, norm_sums, middle_sums, scale_sums
        )
        act_odd = over_seq(act_odd, 1)
        act_near = added(act_even[0], act_odd[0])
        act_far = over_seq(added(act_even[1], act_odd[1]), 2)
        first = added(keep[0], over_y(send_first))
        two = over_y(after(send_two, first))
        out_near = out_sums[0].astype(F32) + out_far[0].astype(F32)
        out_side = added(out_sums[2], out_far[1])
        passed = over_z(after(first, mlp_sums, out_side), 1)
        blocks = [added(added(keep[1], two[0]), passed), added(keep[2], two[1])]
        send_last = over_y(after(send_last, two))
        out_side = over_y(after(out_side, two))
        left, right = over_z(blocks[0], 1), over_z(blocks[1], -1)
        input_grad = last(act_near, act_far, grad_resid, vecs)
        wide_out = exchange_plane(mlp_sums[:wide_rows].reshape(2 * groups, piece_rows, 1024))
        total = added(keep[3], send_last).astype(F32) + left.astype(F32) + right.astype(F32)
        total = after(total, input_grad, wide_out)
        parts = pl.pallas_call(
            prepare_kernel,
            name="prepare",
            out_shape=shaped((4, 48, 768), BF),
            compiler_params=params(),
            cost_estimate=cost(3, 1e6, 1e6),
        )(total)
        parts = lax.all_to_all(parts, "seq", split_axis=0, concat_axis=0, tiled=True)
        sum_qkv, sums = pl.pallas_call(
            finish_kernel,
            name="finish",
            out_shape=[shaped(w_qkv.shape, F32), shaped((8, 128), F32)],
            compiler_params=params(),
            cost_estimate=cost(3, 1e6, 1e6),
        )(parts)
        sums = sums[:, :piece_rows]
        sum_out = jnp.concatenate(
            [total[piece_rows * q : piece_rows * (q + 1), 768:] for q in range(4)], axis=1
        )
        mlp_result = out_near + out_side.astype(F32)
    else:
        packed = even[0]
        grad_proj = attend_back(sect, mixed_grads)
        act_even, act_odd, norm_sums = act_grad(grad_proj, weight_qkv, frame_slots)
        send_first, send_two, send_last, keep = qkv_grad(
            act_one, grad_proj, packed, norm_sums, middle_sums, scale_sums
        )
        act_odd = over_seq(act_odd, 1)
        act_near = added(act_even[0], act_odd[0])
        act_far = over_seq(added(act_even[1], act_odd[1]), 2)
        input_grad = last(act_near, act_far, grad_resid, vecs)
        sums = jnp.concatenate([norm_sums[0:2], middle_sums[0:3], scale_sums[0:1]], axis=0)
        sums = lax.psum(sums, everywhere)
        sums = lax.dynamic_index_in_dim(
            sums.reshape(6, devices, piece_rows), device, 1, keepdims=False
        )
        sends = jnp.concatenate([send_first[None], send_two, send_last[None]])
        full = jnp.stack([keep, sends], axis=1)[:, :, :128, :768].reshape(width, 768)
        sum_qkv = lax.psum_scatter(full, ("z", "y"), scatter_dimension=0, tiled=True)
        sum_qkv = sum_qkv.reshape(groups, piece_rows, 768)
        sum_qkv = lax.all_to_all(sum_qkv, "seq", split_axis=0, concat_axis=0, tiled=True)
        sum_qkv = sum_qkv.reshape(groups, piece_rows, 3, 256).transpose(1, 2, 0, 3)
        sum_qkv = sum_qkv.reshape(w_qkv.shape).astype(F32)
        full = jnp.stack([even[0], odd[0], even[1], odd[1]])
        full = jnp.stack(
            [lax.dynamic_index_in_dim(full, s_here ^ m, 0, keepdims=False) for m in range(4)], axis=1
        ).reshape(width, width)
        sum_out = lax.psum_scatter(full, everywhere, scatter_dimension=0, tiled=True).astype(F32)
        wide_out = exchange_plane(mlp_sums[:wide_rows].reshape(2 * groups, piece_rows, 1024))
        mlp_result = sum(part.astype(F32) for part in send_plane(out_sums))

    layer_out = (resid + mask * vecs[5:6, :] * mlp_result).astype(BF).reshape(frames_in.shape)
    wide_out = wide_out.reshape(2 * groups, piece_rows, 2, depth, units).transpose(1, 2, 3, 0, 4)
    sum_gate_up = wide_out.reshape(w_gate_up.shape).astype(F32)
    sum_down = mlp_sums[wide_rows:].astype(F32)

    return (
        layer_out,
        input_grad,
        sums[0],
        sums[1],
        sum_qkv,
        sum_out,
        sums[4],
        sums[2],
        sums[3],
        sum_gate_up,
        sum_down,
        sums[5],
    )


def solution(mesh):
    clip_groups, groups = mesh.shape["clips"], mesh.shape["seq"]
    depth = clip_groups // 2
    split = Mesh(mesh.devices.reshape(depth, 2, groups), ("z", "y", "seq"))
    clips, everywhere = ("z", "y"), ("z", "y", "seq")
    by_frame, by_clip = P(clips, "seq", None), P(clips)
    by_row, by_entry = P(everywhere, None), P(everywhere)
    return jax.shard_map(
        functools.partial(on_device, rings=depth == 4 and groups == 4),
        mesh=split,
        in_specs=(
            by_frame, by_frame, by_clip, by_clip, by_entry, by_entry, by_row, by_row,
            by_entry, by_entry, by_entry, by_row, by_row, by_entry,
        ),
        out_specs=(
            by_frame, by_frame, by_entry, by_entry, by_row, by_row, by_entry, by_entry,
            by_entry, by_row, by_row, by_entry,
        ),
        check_vma=False,
    )
```
